256 devices in a mesh: wide: 32 (over y, x, core), lon: 8 (over z).
Axes of the slice: x: 4, y: 4, z: 8, core: 2. Of those that a mesh axis runs over, the one named last changes fastest.
Arguments:
- background_ensemble: bfloat16 [256, 256, 2048], P('wide', None, 'lon'), may hold values from -6 to 6
- innov: bfloat16 [256, 256, 2048], P(None, 'wide', 'lon'), may hold values from -6 to 6
- obs_index: int32 [4, 256, 2048], P(None, None, 'lon'), may hold values from 0 to 65535, as said below
- obs_weight: float32 [4, 256, 2048], P(None, None, 'lon'), may hold values from 0.05 to 0.5
- obs_list: int32 [8, 512, 16], P('lon', 'wide'), may hold values from 0 to 23, as said below
- tile_count: int32 [8, 512], P('lon', 'wide'), may hold values from 1 to 16
- taper_class: int32 [8, 512, 16], P('lon', 'wide'), may hold values from 0 to 3
Outputs:
- analysis: bfloat16 [256, 256, 2048], P('wide', None, 'lon')
The draws below stay inside these ranges and needn't reach their ends.
Inputs may be any that keep to these rules, and one draw needn't show every extreme that they name: obs_index[k, i, c] = r * 256 + q names the cell in row r and column q of the observation's own longitude tile, and row r lies among the 8 rows of the region that holds row i. Each row of obs_list names 16 different candidates of its region.
All inputs are finite; a program needn't handle non-finite values.
Results may differ from the reference program's by a relative error of at most 0.0056.
Values may be sent and summed in bfloat16 or wider, within the bound.
A program may use at most 64 MiB of HBM per device.

```python
import jax
import jax.numpy as jnp
from jax import lax

ENSEMBLE_SIZE = 256
LAT_DEV = 8
PATCH_MERIDIANS = 256
BLK = 128
LIST = 16
HALO_BLK = 4
BLOCKS = 16
PARALLEL_LINES = 256
LON = 2048
SB_ALL = 512
TILES = 8
N_WIDE = 32
N_LON = 8


def draw_obs_index(key, part):
    row_ids = lax.broadcasted_iota(jnp.int32, (PARALLEL_LINES, LON), 0)
    col_ids = lax.broadcasted_iota(jnp.int32, (PARALLEL_LINES, LON), 1)
    region = row_ids // LAT_DEV
    extent = (LAT_DEV - 1) * PATCH_MERIDIANS - 1
    anchor = region * (LAT_DEV * PATCH_MERIDIANS) + jax.random.randint(key, (PARALLEL_LINES, LON), 0, extent)
    anchor = jnp.where((row_ids == 0) & (col_ids == 0), 0, anchor)
    anchor = jnp.where((row_ids == PARALLEL_LINES - 1) & (col_ids == 0), PARALLEL_LINES * PATCH_MERIDIANS - PATCH_MERIDIANS - 2, anchor)
    offsets = jnp.array([0, 1, PATCH_MERIDIANS, PATCH_MERIDIANS + 1], jnp.int32)
    return (anchor[None, :, :] + offsets[:, None, None]).astype(jnp.int32)


def draw_obs_list(key, part):
    candidates = BLOCKS + 2 * HALO_BLK
    array_shape = (TILES, SB_ALL, candidates)
    scores = jax.random.randint(key, array_shape, 0, 65536) * candidates + lax.broadcasted_iota(jnp.int32, array_shape, 2)
    ranking = jnp.argsort(scores, axis=-1)
    return ranking[..., :LIST].astype(jnp.int32)


def draw_tile_count(key, part):
    level_key, jitter_key, top_key = jax.random.split(key, 3)
    quarter = LIST // 4
    regions = SB_ALL // BLOCKS
    density = jax.random.randint(level_key, (TILES, regions, 1), 0, 4)
    jitter = jax.random.randint(jitter_key, (TILES, regions, BLOCKS), 0, quarter)
    counts = (1 + quarter * density + jitter).reshape(TILES, SB_ALL)
    top_place = jax.random.randint(top_key, (TILES, 1), 0, SB_ALL)
    low_place = (top_place + BLOCKS) % SB_ALL
    block_ids = lax.broadcasted_iota(jnp.int32, (TILES, SB_ALL), 1)
    counts = jnp.where(block_ids == top_place, LIST, counts)
    counts = jnp.where(block_ids == low_place, 1, counts)
    return counts.astype(jnp.int32)


def with_ends(values, key, smallest, high):
    index_at = [jax.random.randint(jax.random.fold_in(key, axis), (), 0, length) for axis, length in enumerate(values.shape)]
    widest = values.shape.index(max(values.shape))
    beside = index_at[:widest] + [(index_at[widest] + 1) % values.shape[widest]] + index_at[widest + 1:]
    return values.at[tuple(index_at)].set(smallest).at[tuple(beside)].set(high)


def shard_levels(key, dims, shards, least, high):
    def one(dim, blocks):
        heights = jax.random.uniform(jax.random.fold_in(jax.random.fold_in(key, 6), dim), (blocks,), jnp.float32, least / len(shards), high / len(shards))
        return jnp.repeat(jnp.exp(heights), dims[dim] // blocks).reshape((-1,) + (1,) * (len(dims) - dim - 1))

    factor_of = one(*shards[0])
    for cut in shards[1:]:
        factor_of = factor_of * one(*cut)
    return factor_of


def scatter_about(rng, shape, scale, limit, cuts=(), held_as=jnp.bfloat16):
    entries = jax.random.normal(rng, shape, jnp.float32) * scale
    if len(cuts) > 0:
        entries = shard_levels(rng, shape, cuts, -0.22, 0.18) * entries
    return jnp.clip(entries, min=-limit, max=limit).astype(held_as)


def setup_inputs(seed: int = 0) -> dict:
    streams_of = jax.random.split(jax.random.key(seed), 8)
    background_ensemble = scatter_about(streams_of[0], (ENSEMBLE_SIZE, PARALLEL_LINES, LON), 1.0, 6.0, ((0, 32), (2, 8)))
    innov = scatter_about(streams_of[1], (ENSEMBLE_SIZE, PARALLEL_LINES, LON), 1.0, 6.0, ((1, 32), (2, 8)))
    obs_index = draw_obs_index(jax.random.fold_in(streams_of[7], 71), 0)
    obs_weight = jnp.clip(0.05 + 0.45 * jax.random.uniform(streams_of[3], (4, PARALLEL_LINES, LON), jnp.float32) ** shard_levels(streams_of[3], (4, PARALLEL_LINES, LON), ((2, 8),), -0.2, 0.2), 0.05, 0.5)
    obs_list = draw_obs_list(jax.random.fold_in(streams_of[7], 71), 0)
    tile_count = draw_tile_count(jax.random.fold_in(streams_of[7], 71), 0)
    taper_class = with_ends(jax.random.randint(streams_of[6], (TILES, SB_ALL, LIST), 0, 4), jax.random.fold_in(streams_of[6], 1), 0, 3).astype(jnp.int32)
    return dict(background_ensemble=background_ensemble, innov=innov, obs_index=obs_index, obs_weight=obs_weight, obs_list=obs_list, tile_count=tile_count, taper_class=taper_class)


def propagate_model(background_ensemble):
    state_values = background_ensemble.astype(jnp.float32)
    east_neighbour = jnp.roll(state_values, -1, axis=2)
    west_neighbour = jnp.roll(state_values, 1, axis=2)
    northern = jnp.pad(state_values[:, 1:, :], ((0, 0), (0, 1), (0, 0)))
    southern = jnp.pad(state_values[:, :-1, :], ((0, 0), (1, 0), (0, 0)))
    member_spread = east_neighbour + west_neighbour + northern + southern - 4.0 * state_values
    return (state_values + 0.2 * member_spread - 0.3 * (east_neighbour - west_neighbour)).astype(jnp.bfloat16)


def observe(flat, index, weight):
    summed = jnp.zeros((flat.shape[0], index.shape[1]), jnp.float32)
    for k in range(4):
        summed = summed + weight[k][None, :] * jnp.take(flat, index[k], axis=1).astype(jnp.float32)
    return summed.astype(jnp.bfloat16)


def anomaly_from_mean(state_values):
    centred = state_values.astype(jnp.float32)
    return (centred - jnp.mean(centred, axis=-2, keepdims=True)).astype(jnp.bfloat16)


def taper_tiles(classes, in_use, tile_width):
    row_ids = lax.broadcasted_iota(jnp.float32, (tile_width, tile_width), 0)
    col_ids = lax.broadcasted_iota(jnp.float32, (tile_width, tile_width), 1)
    offset = row_ids - col_ids
    length = 8.0 * jnp.exp2(classes.astype(jnp.float32))
    scaled = offset / length[..., None, None]
    return in_use[..., None, None] / (1.0 + scaled * scaled)


def partition_patches(grid):
    shaped = grid.reshape(ENSEMBLE_SIZE, N_WIDE, LAT_DEV, N_LON, PATCH_MERIDIANS).transpose(3, 1, 0, 2, 4)
    return shaped.reshape(N_LON, N_WIDE, ENSEMBLE_SIZE, LAT_DEV * PATCH_MERIDIANS)


def widen_regions(regions):
    blocks = regions.reshape(N_LON, N_WIDE, ENSEMBLE_SIZE, BLOCKS, BLK)
    west_neighbour = jnp.roll(blocks, 1, axis=0)[:, :, :, BLOCKS - HALO_BLK:]
    east_neighbour = jnp.roll(blocks, -1, axis=0)[:, :, :, :HALO_BLK]
    return jnp.concatenate([west_neighbour, blocks, east_neighbour], axis=3)


def update_region(inputs):
    model_anomaly, anchor, cand_obs, cand_innov, lists, counts, classes = inputs
    state_tile = model_anomaly.reshape(ENSEMBLE_SIZE, BLOCKS, BLK).astype(jnp.float32)
    picked_obs = jnp.take(cand_obs, lists, axis=1).astype(jnp.float32)
    picked_innov = jnp.take(cand_innov, lists, axis=1).astype(jnp.float32)
    in_use = (jnp.arange(LIST, dtype=jnp.int32)[None, :] < counts[:, None]).astype(jnp.float32)
    covariance = jnp.einsum('mbc,mbjo->bjco', state_tile, picked_obs) / (ENSEMBLE_SIZE - 1.0)
    tapered = (covariance * taper_tiles(classes, in_use, BLK)).astype(jnp.bfloat16)
    tapered = lax.optimization_barrier(tapered).astype(jnp.float32)
    change = jnp.einsum('mbjo,bjco->mbc', picked_innov, tapered)
    return (anchor.astype(jnp.float32) + change.reshape(ENSEMBLE_SIZE, BLOCKS * BLK)).astype(jnp.bfloat16)


def reference(background_ensemble, innov, obs_index, obs_weight, obs_list, tile_count, taper_class):
    prediction_increment = propagate_model(background_ensemble)
    zonal_bands = prediction_increment.reshape(ENSEMBLE_SIZE, PARALLEL_LINES, N_LON, PATCH_MERIDIANS).transpose(2, 0, 1, 3).reshape(N_LON, ENSEMBLE_SIZE, PARALLEL_LINES * PATCH_MERIDIANS)
    strip_index = obs_index.reshape(4, PARALLEL_LINES, N_LON, PATCH_MERIDIANS).transpose(2, 0, 1, 3).reshape(N_LON, 4, PARALLEL_LINES * PATCH_MERIDIANS)
    strip_weight = obs_weight.reshape(4, PARALLEL_LINES, N_LON, PATCH_MERIDIANS).transpose(2, 0, 1, 3).reshape(N_LON, 4, PARALLEL_LINES * PATCH_MERIDIANS)
    observed = lax.map(lambda a: observe(a[0], a[1], a[2]), (zonal_bands, strip_index, strip_weight))
    obs_regions = observed.reshape(N_LON, ENSEMBLE_SIZE, N_WIDE, LAT_DEV * PATCH_MERIDIANS).transpose(0, 2, 1, 3)
    predicted_patches = partition_patches(prediction_increment)
    model_anomaly = anomaly_from_mean(predicted_patches)
    obs_dev = anomaly_from_mean(obs_regions)
    cand_obs = widen_regions(obs_dev)
    cand_innov = widen_regions(partition_patches(innov))
    total_tally = N_LON * N_WIDE
    patch_gridpoints = LAT_DEV * PATCH_MERIDIANS
    candidates = BLOCKS + 2 * HALO_BLK
    updated = lax.map(update_region, (
        model_anomaly.reshape(total_tally, ENSEMBLE_SIZE, patch_gridpoints),
        predicted_patches.reshape(total_tally, ENSEMBLE_SIZE, patch_gridpoints),
        cand_obs.reshape(total_tally, ENSEMBLE_SIZE, candidates, BLK),
        cand_innov.reshape(total_tally, ENSEMBLE_SIZE, candidates, BLK),
        obs_list.reshape(total_tally, BLOCKS, LIST),
        tile_count.reshape(total_tally, BLOCKS),
        taper_class.reshape(total_tally, BLOCKS, LIST)))
    shaped = updated.reshape(N_LON, N_WIDE, ENSEMBLE_SIZE, LAT_DEV, PATCH_MERIDIANS).transpose(2, 1, 3, 0, 4)
    return shaped.reshape(ENSEMBLE_SIZE, PARALLEL_LINES, LON)
```

```python
import functools

import jax
import jax.numpy as jnp
from jax import lax
from jax.experimental import pallas as pl
from jax.experimental.pallas import tpu as pltpu
from jax.sharding import PartitionSpec as P

MESH = pl.DeviceIdType.MESH
F32 = jnp.float32
BF16 = jnp.bfloat16

M = 256
ROWS = 8
Q = 256
NW = 32
NL = 8
MD = 8
BLK = 128
HALO = 512
CELLS = ROWS * Q
CAND = CELLS + 2 * HALO
PAIR = 2
CHUNKS = ROWS // PAIR


def iota(shape, dim):
    return lax.broadcasted_iota(jnp.int32, shape, dim)


def kernel(
    x_hbm, innov_hbm, idx_hbm, wgt_hbm, list_ref, count_ref, class_ref, out_ref,
    x_in, x_f, edge_out, edge_in, sent, region, innov_in, innov_all, idx, wgt, cols, sel,
    dev, obs_acc, obs_all, table, dense_v, dense_s, tapered, back, home,
    load_sem, edge_send, edge_recv, a_send, a_recv, ih_send, ih_recv, oh_send, oh_recv,
    b_send, b_recv, class_sem,
):
    me = lax.axis_index("wide")
    tile = lax.axis_index("lon")
    east = lax.rem(tile + 1, NL)
    west = lax.rem(tile + NL - 1, NL)

    load_x = pltpu.make_async_copy(x_hbm, x_in, load_sem.at[0])
    load_x.start()
    load_innov = pltpu.make_async_copy(innov_hbm, innov_in, load_sem.at[1])
    load_innov.start()
    first = pl.multiple_of(me * ROWS, ROWS)
    load_idx = pltpu.make_async_copy(idx_hbm.at[:, pl.ds(first, ROWS), :], idx, load_sem.at[2])
    load_idx.start()
    load_wgt = pltpu.make_async_copy(wgt_hbm.at[:, pl.ds(first, ROWS), :], wgt, load_sem.at[3])
    load_wgt.start()

    barrier = pltpu.get_barrier_semaphore()

    def greet(k, carry):
        other = lax.rem(me + k, NW)
        pl.semaphore_signal(barrier, inc=1, device_id={"wide": other}, device_id_type=MESH)
        return carry

    for t in (east, west):
        pl.semaphore_signal(barrier, inc=1, device_id={"lon": t}, device_id_type=MESH)
    lax.fori_loop(1, NW, greet, 0)

    load_x.wait()
    x_f[:, 0:8, :] = jnp.zeros((MD, 8, Q), F32)
    x_f[:, 8 + 256:8 + 256 + 8, :] = jnp.zeros((MD, 8, Q), F32)

    def widen(step, carry):
        r0 = pl.multiple_of(step * 32, 32)
        lane = iota((32, BLK), 1)
        left = jnp.zeros((32, BLK), F32)
        right = jnp.zeros((32, BLK), F32)
        for m in range(MD):
            v = x_in[m, pl.ds(r0, 32), :].astype(F32)
            x_f[m, pl.ds(pl.multiple_of(r0 + 8, 8), 32), :] = v
            a = v[:, :BLK]
            b = v[:, BLK:]
            left = jnp.where(lane == m, pltpu.roll(a, m, 1) if m else a, left)
            right = jnp.where(lane == m, pltpu.roll(b, m + 1, 1), right)
        edge_out[0, pl.ds(r0, 32), :] = left.astype(BF16)
        edge_out[1, pl.ds(r0, 32), :] = right.astype(BF16)
        return carry

    lax.fori_loop(0, 8, widen, 0)

    pl.semaphore_wait(barrier, NW - 1 + 2)

    edges = []
    for side, t in ((0, west), (1, east)):
        copy = pltpu.make_async_remote_copy(
            src_ref=edge_out.at[side], dst_ref=edge_in.at[side],
            send_sem=edge_send.at[side], recv_sem=edge_recv.at[side],
            device_id={"lon": t}, device_id_type=MESH)
        copy.start()
        edges.append(copy)

    d = (iota((BLK, BLK), 0) - iota((BLK, BLK), 1)).astype(F32)
    for c in range(4):
        s = d * (1.0 / (8.0 * 2.0 ** c))
        table[c] = (1.0 / (M - 1.0)) / (1.0 + s * s)
    table[4] = jnp.zeros((BLK, BLK), F32)

    block = iota((16, BLK), 0)
    ids = iota((16, BLK), 1)
    counts = jnp.zeros((16, BLK), jnp.int32)
    for b in range(16):
        counts = jnp.where(block == b, count_ref[0, b], counts)
    listed = list_ref[0]
    classes = class_ref[0]
    dense = jnp.full((16, BLK), 4, jnp.int32)
    for j in range(16):
        hit = (ids == listed[:, j:j + 1]) & (counts > j)
        dense = jnp.where(hit, classes[:, j:j + 1], dense)
    dense_v[...] = dense
    to_scalar = pltpu.make_async_copy(dense_v, dense_s, class_sem)
    to_scalar.start()

    for copy in edges:
        copy.wait()

    def forecast(r, carry):
        r0 = pl.multiple_of(r * ROWS, ROWS)
        lane = iota((ROWS, BLK), 1)
        e_in = edge_in[0, pl.ds(pl.multiple_of(lax.div(r, 2) * 16, 16), 16), :].astype(F32)
        w_in = edge_in[1, pl.ds(pl.multiple_of(lax.div(r, 2) * 16, 16), 16), :].astype(F32)
        odd = lax.rem(r, 2) == 1
        e_in = jnp.where(odd, e_in[8:16], e_in[0:8])
        w_in = jnp.where(odd, w_in[8:16], w_in[0:8])
        halves = [[], []]
        for m in range(MD):
            around = x_f[m, pl.ds(r0, 3 * ROWS), :]
            v, n, s = around[8:16], around[9:17], around[7:15]
            a, b = v[:, :BLK], v[:, BLK:]
            a_up, b_up = pltpu.roll(a, BLK - 1, 1), pltpu.roll(b, BLK - 1, 1)
            a_dn, b_dn = pltpu.roll(a, 1, 1), pltpu.roll(b, 1, 1)
            e_edge = pltpu.roll(e_in, BLK - 1 - m, 1)
            w_edge = pltpu.roll(w_in, (BLK - m) % BLK, 1) if m else w_in
            e_a = jnp.where(lane == BLK - 1, b_up, a_up)
            e_b = jnp.where(lane == BLK - 1, e_edge, b_up)
            w_a = jnp.where(lane == 0, w_edge, a_dn)
            w_b = jnp.where(lane == 0, a_dn, b_dn)
            for h, (c, e, w) in enumerate(((a, e_a, w_a), (b, e_b, w_b))):
                hs = slice(h * BLK, (h + 1) * BLK)
                spread = e + w + n[:, hs] + s[:, hs] - 4.0 * c
                halves[h].append(c + 0.2 * spread - 0.3 * (e - w))
        pieces = [jnp.transpose(jnp.stack(h, axis=0), (1, 0, 2)) for h in halves]
        sent[r] = jnp.concatenate(pieces, axis=1).astype(BF16)
        return carry

    lax.fori_loop(0, NW, forecast, 0)

    own = []
    for j in range(CHUNKS):
        rows = pl.ds(j * PAIR, PAIR)
        copy = pltpu.make_async_copy(sent.at[me, rows], region.at[me, rows], a_recv.at[j])
        copy.start()

        def send(k, carry, rows=rows, j=j):
            other = lax.rem(me + k, NW)
            pltpu.make_async_remote_copy(
                src_ref=sent.at[other, rows], dst_ref=region.at[me, rows],
                send_sem=a_send.at[j], recv_sem=a_recv.at[j],
                device_id={"wide": other}, device_id_type=MESH).start()
            return carry

        lax.fori_loop(1, NW, send, 0)

    load_innov.wait()

    def turn(g, carry):
        m0 = pl.multiple_of(g * 16, 16)
        v = innov_in[pl.ds(m0, 16)].astype(F32)
        parts = [jnp.transpose(v[:8], (1, 0, 2)), jnp.transpose(v[8:], (1, 0, 2))]
        u = jnp.concatenate(parts, axis=1).astype(BF16)
        for r in range(ROWS):
            innov_all[pl.ds(m0, 16), HALO + r * Q:HALO + (r + 1) * Q] = u[r]
        return carry

    lax.fori_loop(0, M // 16, turn, 0)

    def lon_copy(src, dst, send_sem, recv_sem, t):
        copy = pltpu.make_async_remote_copy(
            src_ref=src, dst_ref=dst, send_sem=send_sem, recv_sem=recv_sem,
            device_id={"lon": t}, device_id_type=MESH)
        copy.start()
        return copy

    innov_halo = [
        lon_copy(innov_all.at[:, pl.ds(CELLS, HALO)], innov_all.at[:, pl.ds(0, HALO)],
                 ih_send.at[0], ih_recv.at[0], east),
        lon_copy(innov_all.at[:, pl.ds(HALO, HALO)], innov_all.at[:, pl.ds(HALO + CELLS, HALO)],
                 ih_send.at[1], ih_recv.at[1], west),
    ]

    load_idx.wait()
    load_wgt.wait()
    origin = me * CELLS

    def columns(i, carry):
        parts = [(idx[k, pl.ds(i, 1), :] - origin).astype(F32) for k in range(4)]
        parts += [wgt[k, pl.ds(i, 1), :] for k in range(4)]
        stacked = jnp.concatenate(parts + [jnp.zeros((BLK - 8, Q), F32)], axis=0)
        cols[pl.ds(pl.multiple_of(i * Q, Q), Q), :] = jnp.transpose(stacked, (1, 0))
        return carry

    lax.fori_loop(0, ROWS, columns, 0)

    def select(g, carry):
        o0 = pl.multiple_of(g * 16, 16)
        here = cols[pl.ds(o0, 16), :]
        cell = [jnp.broadcast_to(here[:, k:k + 1], (16, BLK)) for k in range(4)]
        weight = [jnp.broadcast_to(here[:, 4 + k:5 + k], (16, BLK)) for k in range(4)]
        ids = iota((16, BLK), 1).astype(F32)
        for t in range(CELLS // BLK):
            at = ids + float(t * BLK)
            acc = jnp.where(at == cell[0], weight[0], 0.0)
            for k in range(1, 4):
                acc = acc + jnp.where(at == cell[k], weight[k], 0.0)
            sel[pl.ds(o0, 16), t * BLK:(t + 1) * BLK] = acc.astype(BF16)
        return carry

    lax.fori_loop(0, CELLS // 16, select, 0)

    def anomaly(r):
        v = region[:, r].astype(F32)
        for h in range(2):
            u = v[:, h * MD:(h + 1) * MD, :].reshape(M, BLK)
            u = u - jnp.sum(u, axis=0, keepdims=True) * (1.0 / M)
            dev[:, r * Q + h * BLK:r * Q + (h + 1) * BLK] = u.astype(BF16)

    def partial_obs(j, o):
        cells = slice(j * PAIR * Q, (j + 1) * PAIR * Q)
        return lax.dot_general(
            sel[pl.ds(pl.multiple_of(o * Q, Q), Q), cells], dev[:, cells],
            (((1,), (1,)), ((), ())), preferred_element_type=F32)

    for j in range(CHUNKS):
        rows = pl.ds(j * PAIR, PAIR)
        pltpu.make_async_copy(region.at[:, rows], region.at[:, rows], a_recv.at[j]).wait()
        for r in range(j * PAIR, (j + 1) * PAIR):
            anomaly(r)
        if j < CHUNKS - 1:
            def add(o, carry, j=j):
                at = pl.ds(pl.multiple_of(o * Q, Q), Q)
                part = partial_obs(j, o)
                obs_acc[at, :] = part if j == 0 else obs_acc[at, :] + part
                return carry

            lax.fori_loop(0, ROWS, add, 0)

    def finish(o, carry):
        at = pl.ds(pl.multiple_of(o * Q, Q), Q)
        to = pl.ds(pl.multiple_of(o * Q + HALO, Q), Q)
        obs_all[to, :] = (obs_acc[at, :] + partial_obs(CHUNKS - 1, o)).astype(BF16)
        return carry

    lax.fori_loop(0, 2, finish, 0)
    lax.fori_loop(ROWS - 2, ROWS, finish, 0)
    obs_halo = [
        lon_copy(obs_all.at[pl.ds(CELLS, HALO)], obs_all.at[pl.ds(0, HALO)],
                 oh_send.at[0], oh_recv.at[0], east),
        lon_copy(obs_all.at[pl.ds(HALO, HALO)], obs_all.at[pl.ds(HALO + CELLS, HALO)],
                 oh_send.at[1], oh_recv.at[1], west),
    ]
    lax.fori_loop(2, ROWS - 2, finish, 0)

    for copy in innov_halo + obs_halo:
        copy.wait()
    to_scalar.wait()

    def update(r, carry):
        c0 = pl.multiple_of(r * Q, Q)
        right = dev[:, pl.ds(c0, Q)]
        for i in range(CAND // Q):
            cov = jnp.dot(obs_all[i * Q:(i + 1) * Q, :], right, preferred_element_type=F32)
            for oh in range(2):
                for ch in range(2):
                    factor = table[dense_s[2 * r + ch, 2 * i + oh]]
                    part = cov[oh * BLK:(oh + 1) * BLK, ch * BLK:(ch + 1) * BLK] * factor
                    tapered[i * Q + oh * BLK:i * Q + (oh + 1) * BLK, ch * BLK:(ch + 1) * BLK] = part.astype(BF16)
        change = jnp.dot(innov_all[...], tapered[...], preferred_element_type=F32)
        state = region[:, r].astype(F32)
        parts = [
            state[:, h * MD:(h + 1) * MD, :] + change[:, h * BLK:(h + 1) * BLK].reshape(NW, MD, BLK)
            for h in range(2)
        ]
        back[:, r] = jnp.concatenate(parts, axis=1).astype(BF16)
        pltpu.make_async_copy(back.at[me, r], home.at[me, r], b_recv).start()

        def send(k, inner):
            other = lax.rem(me + k, NW)
            pltpu.make_async_remote_copy(
                src_ref=back.at[other, r], dst_ref=home.at[me, r],
                send_sem=b_send, recv_sem=b_recv,
                device_id={"wide": other}, device_id_type=MESH).start()
            return inner

        lax.fori_loop(1, NW, send, 0)
        return carry

    lax.fori_loop(0, ROWS, update, 0)

    pltpu.make_async_copy(home, home, b_recv).wait()

    def settle(g, carry):
        v = home[pl.ds(2 * g, 2)].astype(F32)
        for h in range(2):
            u = v[:, :, h * MD:(h + 1) * MD, :]
            parts = [jnp.transpose(u[0], (1, 0, 2)), jnp.transpose(u[1], (1, 0, 2))]
            out_ref[:, pl.ds(pl.multiple_of(g * 16, 16), 16), h * BLK:(h + 1) * BLK] = (
                jnp.concatenate(parts, axis=1).astype(BF16))
        return carry

    lax.fori_loop(0, NW // 2, settle, 0)

    for j in range(CHUNKS):
        rows = pl.ds(j * PAIR, PAIR)
        some = sent.at[pl.ds(0, NW - 1), rows]
        pltpu.make_async_copy(some, some, a_send.at[j]).wait()
    some = back.at[pl.ds(0, NW - 1)]
    pltpu.make_async_copy(some, some, b_send).wait()


def body(x, innov, obs_index, obs_weight, obs_list, tile_count, taper_class):
    anywhere = pl.BlockSpec(memory_space=pl.ANY)
    vmem = pl.BlockSpec(memory_space=pltpu.VMEM)
    dma = pltpu.SemaphoreType.DMA
    return pl.pallas_call(
        kernel,
        out_shape=jax.ShapeDtypeStruct((MD, 256, Q), BF16),
        in_specs=[anywhere] * 4 + [vmem, pl.BlockSpec(memory_space=pltpu.SMEM), vmem],
        out_specs=vmem,
        scratch_shapes=[
            pltpu.VMEM((MD, 256, Q), BF16),
            pltpu.VMEM((MD, 256 + 16, Q), F32),
            pltpu.VMEM((2, 256, BLK), BF16),
            pltpu.VMEM((2, 256, BLK), BF16),
            pltpu.VMEM((NW, ROWS, 16, BLK), BF16),
            pltpu.VMEM((NW, ROWS, 16, BLK), BF16),
            pltpu.VMEM((M, ROWS, Q), BF16),
            pltpu.VMEM((M, CAND), BF16),
            pltpu.VMEM((4, ROWS, Q), jnp.int32),
            pltpu.VMEM((4, ROWS, Q), F32),
            pltpu.VMEM((CELLS, BLK), F32),
            pltpu.VMEM((CELLS, CELLS), BF16),
            pltpu.VMEM((M, CELLS), BF16),
            pltpu.VMEM((CELLS, M), F32),
            pltpu.VMEM((CAND, M), BF16),
            pltpu.VMEM((5, BLK, BLK), F32),
            pltpu.VMEM((16, BLK), jnp.int32),
            pltpu.SMEM((16, BLK), jnp.int32),
            pltpu.VMEM((CAND, Q), BF16),
            pltpu.VMEM((NW, ROWS, 16, BLK), BF16),
            pltpu.VMEM((NW, ROWS, 16, BLK), BF16),
            dma((4,)), dma((2,)), dma((2,)), dma((CHUNKS,)), dma((CHUNKS,)),
            dma((2,)), dma((2,)), dma((2,)), dma((2,)), dma, dma, dma,
        ],
        compiler_params=pltpu.CompilerParams(
            collective_id=0, has_side_effects=True, vmem_limit_bytes=56 * 1024 * 1024),
    )(x, innov, obs_index, obs_weight, obs_list, tile_count, taper_class)


def solution(mesh):
    in_specs = (
        P("wide", None, "lon"),
        P(None, "wide", "lon"),
        P(None, None, "lon"),
        P(None, None, "lon"),
        P("lon", "wide", None),
        P("lon", "wide"),
        P("lon", "wide", None),
    )
    return jax.shard_map(
        body, mesh=mesh, in_specs=in_specs, out_specs=P("wide", None, "lon"), check_vma=False)
```

```python
import functools

import jax
import jax.numpy as jnp
from jax import lax
from jax.experimental import pallas as pl
from jax.experimental.pallas import tpu as pltpu
from jax.sharding import PartitionSpec as P

MESH = pl.DeviceIdType.MESH
F32 = jnp.float32
BF16 = jnp.bfloat16

M = 256
ROWS = 8
Q = 256
NW = 32
NL = 8
MD = 8
BLK = 128
HALO = 512
CELLS = ROWS * Q
CAND = CELLS + 2 * HALO
CHUNKS = ((0, 4), (4, 4))
OFFSETS = (10, 9, 11, 6, 14, 5, 7, 13, 15, 2, 8, 1, 3, 4, 12)
GROUP = 64


def iota(shape, dim):
    return lax.broadcasted_iota(jnp.int32, shape, dim)


def kernel(
    x_hbm, innov_hbm, idx_hbm, wgt_hbm, list_hbm, count_hbm, class_hbm, home,
    x_in, x_f, edge_out, edge_in, edge_f, sent, region, innov_in, innov_all, idx, wgt, cols, sel,
    dev, obs_acc, obs_all, table, listed, classes, count_s, dense_v, dense_s,
    own0, own1, out0, out1, part, back,
    load_sem, edge_send, edge_recv, a_send, a_recv, ih_send, ih_recv, oh_send, oh_recv,
    b_send, b_recv, class_sem,
):
    me = lax.axis_index("wide")
    tile = lax.axis_index("lon")
    east = lax.rem(tile + 1, NL)
    west = lax.rem(tile + NL - 1, NL)
    core = lax.rem(me, 2)
    my_x = lax.rem(lax.div(me, 2), 4)
    my_y = lax.div(me, 8)

    def chip(k):
        code = jnp.int32(OFFSETS[0])
        for i in range(1, len(OFFSETS)):
            code = jnp.where(k == i, OFFSETS[i], code)
        to_x = lax.rem(my_x + lax.rem(code, 4), 4)
        to_y = lax.rem(my_y + lax.div(code, 4), 4)
        return to_y * 8 + to_x * 2

    first = pl.multiple_of(me * ROWS, ROWS)
    loads = [
        pltpu.make_async_copy(src, dst, load_sem.at[i]) for i, (src, dst) in enumerate((
            (x_hbm, x_in),
            (idx_hbm.at[:, pl.ds(first, ROWS), :], idx),
            (wgt_hbm.at[:, pl.ds(first, ROWS), :], wgt),
            (innov_hbm, innov_in),
            (list_hbm, listed),
            (count_hbm, count_s),
            (class_hbm, classes),
        ))
    ]
    load_x, load_idx, load_wgt, load_innov, load_list, load_count, load_class = loads
    for load in loads:
        load.start()

    barrier = pltpu.get_barrier_semaphore()

    def greet(k, carry):
        other = lax.rem(me + k, NW)
        pl.semaphore_signal(barrier, inc=1, device_id={"wide": other}, device_id_type=MESH)
        return carry

    for t in (east, west):
        pl.semaphore_signal(barrier, inc=1, device_id={"lon": t}, device_id_type=MESH)
    lax.fori_loop(1, NW, greet, 0)

    x_f[:, 0:8, :] = jnp.zeros((MD, 8, Q), F32)
    x_f[:, 8 + 256:8 + 256 + 8, :] = jnp.zeros((MD, 8, Q), F32)
    load_x.wait()

    def widen(g, carry):
        left, right = carry
        r0 = pl.multiple_of(g * 32, 32)
        lane = iota((32, BLK), 1) - g * 8
        a_new = jnp.zeros((32, BLK), F32)
        b_new = jnp.zeros((32, BLK), F32)
        lane0 = iota((32, BLK), 1)
        for m in range(MD):
            v = x_in[m, pl.ds(r0, 32), :].astype(F32)
            x_f[m, pl.ds(pl.multiple_of(r0 + 8, 8), 32), :] = v
            a = v[:, :BLK]
            b = v[:, BLK:]
            a_new = jnp.where(lane0 == m, pltpu.roll(a, m, 1) if m else a, a_new)
            b_new = jnp.where(lane0 == m, pltpu.roll(b, m + 1, 1), b_new)
        here = (lane >= 0) & (lane < MD)
        left = jnp.where(here, pltpu.roll(a_new, g * 8, 1), left)
        right = jnp.where(here, pltpu.roll(b_new, g * 8, 1), right)
        return left, right

    zeros = jnp.zeros((32, BLK), F32)
    left, right = lax.fori_loop(0, 8, widen, (zeros, zeros))
    edge_out[0] = left.astype(BF16)
    edge_out[1] = right.astype(BF16)

    d = (iota((BLK, BLK), 0) - iota((BLK, BLK), 1)).astype(F32)
    for c in range(4):
        s = d * (1.0 / (8.0 * 2.0 ** c))
        table[c] = (1.0 / (M - 1.0)) / (1.0 + s * s)
    table[4] = jnp.zeros((BLK, BLK), F32)

    load_idx.wait()
    load_wgt.wait()
    origin = me * CELLS

    def columns(i, carry):
        parts = [(idx[k, pl.ds(i, 1), :] - origin).astype(F32) for k in range(4)]
        parts += [wgt[k, pl.ds(i, 1), :] for k in range(4)]
        stacked = jnp.concatenate(parts + [jnp.zeros((BLK - 8, Q), F32)], axis=0)
        cols[pl.ds(pl.multiple_of(i * Q, Q), Q), :] = jnp.transpose(stacked, (1, 0))
        return carry

    lax.fori_loop(0, ROWS, columns, 0, unroll=2)

    pl.semaphore_wait(barrier, NW - 1 + 2)

    def lon_copy(src, dst, send_sem, recv_sem, t):
        copy = pltpu.make_async_remote_copy(
            src_ref=src, dst_ref=dst, send_sem=send_sem, recv_sem=recv_sem,
            device_id={"lon": t}, device_id_type=MESH)
        copy.start()
        return copy

    edges = [
        lon_copy(edge_out.at[side], edge_in.at[side], edge_send.at[side], edge_recv.at[side], t)
        for side, t in ((0, west), (1, east))
    ]

    load_innov.wait()

    def turn(g, carry):
        m0 = pl.multiple_of(g * 16, 16)
        v = innov_in[pl.ds(m0, 16)].astype(F32)
        parts = [jnp.transpose(v[:8], (1, 0, 2)), jnp.transpose(v[8:], (1, 0, 2))]
        u = jnp.concatenate(parts, axis=1).astype(BF16)
        for r in range(ROWS):
            innov_all[pl.ds(m0, 16), HALO + r * Q:HALO + (r + 1) * Q] = u[r]
        return carry

    lax.fori_loop(0, M // 16, turn, 0)
    innov_halo = [
        lon_copy(innov_all.at[:, pl.ds(CELLS, HALO)], innov_all.at[:, pl.ds(0, HALO)],
                 ih_send.at[0], ih_recv.at[0], east),
        lon_copy(innov_all.at[:, pl.ds(HALO, HALO)], innov_all.at[:, pl.ds(HALO + CELLS, HALO)],
                 ih_send.at[1], ih_recv.at[1], west),
    ]

    for load in (load_list, load_count, load_class):
        load.wait()
    block = iota((16, BLK), 0)
    ids = iota((16, BLK), 1)
    counts = jnp.zeros((16, BLK), jnp.int32)
    for b in range(16):
        counts = jnp.where(block == b, count_s[0, b], counts)
    dense = jnp.full((16, BLK), 4, jnp.int32)
    for j in range(16):
        hit = (ids == listed[0, :, j:j + 1]) & (counts > j)
        dense = jnp.where(hit, classes[0, :, j:j + 1], dense)
    dense_v[...] = dense
    to_scalar = pltpu.make_async_copy(dense_v, dense_s, class_sem)
    to_scalar.start()

    def select(g, carry):
        o0 = pl.multiple_of(g * GROUP, GROUP)
        here = cols[pl.ds(o0, GROUP), :]
        cell = [jnp.broadcast_to(here[:, k:k + 1], (GROUP, BLK)).astype(jnp.int32) for k in range(4)]
        row = [lax.shift_right_logical(c, 8).astype(F32).astype(BF16) for c in cell]
        col = [(c & (Q - 1)).astype(F32).astype(BF16) for c in cell]
        weight = [jnp.broadcast_to(here[:, 4 + k:5 + k], (GROUP, BLK)).astype(BF16) for k in range(4)]
        lanes = iota((GROUP, BLK), 1).astype(F32)
        none = jnp.zeros((GROUP, BLK), BF16)
        for r in range(ROWS):
            w = [jnp.where(row[k] == jnp.bfloat16(r), weight[k], none) for k in range(4)]
            for h in range(2):
                at = (lanes + float(h * BLK)).astype(BF16)
                acc = jnp.where(at == col[0], w[0], none)
                for k in range(1, 4):
                    acc = acc + jnp.where(at == col[k], w[k], none)
                sel[pl.ds(o0, GROUP), r * Q + h * BLK:r * Q + (h + 1) * BLK] = acc
        return carry

    steps = CELLS // GROUP
    lax.fori_loop(0, steps // 4, select, 0)

    for copy in edges:
        copy.wait()
    edge_f[...] = edge_in[...].astype(F32)

    def forecast(r):
        r0 = pl.multiple_of(r * ROWS, ROWS)
        lane = iota((ROWS, BLK), 1)
        sub = pl.ds(pl.multiple_of(lax.rem(r, 4) * ROWS, ROWS), ROWS)
        turns = lax.rem(BLK - lax.div(r, 4) * 8, BLK)
        e_in = pltpu.roll(edge_f[0, sub, :], turns, 1)
        w_in = pltpu.roll(edge_f[1, sub, :], turns, 1)
        halves = [[], []]
        for m in range(MD):
            around = x_f[m, pl.ds(r0, 3 * ROWS), :]
            v, n, s = around[8:16], around[9:17], around[7:15]
            a, b = v[:, :BLK], v[:, BLK:]
            a_up, b_up = pltpu.roll(a, BLK - 1, 1), pltpu.roll(b, BLK - 1, 1)
            a_dn, b_dn = pltpu.roll(a, 1, 1), pltpu.roll(b, 1, 1)
            e_edge = pltpu.roll(e_in, BLK - 1 - m, 1)
            w_edge = pltpu.roll(w_in, BLK - m, 1) if m else w_in
            e_a = jnp.where(lane == BLK - 1, b_up, a_up)
            e_b = jnp.where(lane == BLK - 1, e_edge, b_up)
            w_a = jnp.where(lane == 0, w_edge, a_dn)
            w_b = jnp.where(lane == 0, a_dn, b_dn)
            for h, (c, e, w) in enumerate(((a, e_a, w_a), (b, e_b, w_b))):
                hs = slice(h * BLK, (h + 1) * BLK)
                spread = e + w + n[:, hs] + s[:, hs] - 4.0 * c
                halves[h].append(c + 0.2 * spread - 0.3 * (e - w))
        pieces = [jnp.transpose(jnp.stack(h, axis=0), (1, 0, 2)) for h in halves]
        sent[r] = jnp.concatenate(pieces, axis=1).astype(BF16)

    def send_forecast(other, j):
        rows = pl.ds(*CHUNKS[j])
        pltpu.make_async_remote_copy(
            src_ref=sent.at[other, rows], dst_ref=region.at[me, rows],
            send_sem=a_send.at[j], recv_sem=a_recv.at[j],
            device_id={"wide": other}, device_id_type=MESH).start()

    def send_near(other, c, j):
        rows = pl.ds(*CHUNKS[j])

        @pl.when(core == c)
        def _():
            pltpu.make_async_copy(sent.at[me, rows], region.at[me, rows], a_recv.at[j]).start()

        @pl.when(core != c)
        def _():
            send_forecast(other, j)

    for c in range(2):
        def compute_send(k, carry, c=c):
            other = chip(k) + c
            forecast(other)
            send_forecast(other, 0)
            return carry

        lax.fori_loop(0, len(OFFSETS), compute_send, 0)
        near = lax.div(me, 2) * 2 + c
        forecast(near)
        sibling = lax.div(me, 2) * 2 + 1 - core
        send_near(sibling, c, 0)
        for j in range(1, len(CHUNKS)):
            def send_rest(k, carry, c=c, j=j):
                send_forecast(chip(k) + c, j)
                return carry

            lax.fori_loop(0, len(OFFSETS), send_rest, 0)
            send_near(sibling, c, j)

    lax.fori_loop(steps // 4, steps, select, 0, unroll=2)

    def anomaly(r):
        v = region[:, r].astype(F32)
        for h in range(2):
            u = v[:, h * MD:(h + 1) * MD, :].reshape(M, BLK)
            u = u - jnp.sum(u, axis=0, keepdims=True) * (1.0 / M)
            dev[:, r * Q + h * BLK:r * Q + (h + 1) * BLK] = u.astype(BF16)

    for j, (row0, rows) in enumerate(CHUNKS):
        arrived = region.at[:, pl.ds(row0, rows)]
        pltpu.make_async_copy(arrived, arrived, a_recv.at[j]).wait()
        for r in range(row0, row0 + rows):
            anomaly(r)
        cells = slice(row0 * Q, (row0 + rows) * Q)

        def product(o0, n, cells=cells):
            return lax.dot_general(
                sel[o0:o0 + n, cells], dev[:, cells],
                (((1,), (1,)), ((), ())), preferred_element_type=F32)

        if j == 0:
            obs_acc[...] = product(0, CELLS)
        elif j < len(CHUNKS) - 1:
            obs_acc[...] += product(0, CELLS)
        else:
            for o0 in (0, CELLS - HALO):
                total = obs_acc[o0:o0 + HALO, :] + product(o0, HALO)
                obs_all[HALO + o0:HALO + o0 + HALO, :] = total.astype(BF16)
            obs_halo = [
                lon_copy(obs_all.at[pl.ds(CELLS, HALO)], obs_all.at[pl.ds(0, HALO)],
                         oh_send.at[0], oh_recv.at[0], east),
                lon_copy(obs_all.at[pl.ds(HALO, HALO)], obs_all.at[pl.ds(HALO + CELLS, HALO)],
                         oh_send.at[1], oh_recv.at[1], west),
            ]
            total = obs_acc[HALO:CELLS - HALO, :] + product(HALO, CELLS - 2 * HALO)
            obs_all[2 * HALO:CELLS, :] = total.astype(BF16)

    to_scalar.wait()

    def covariance(r, candidates, tapered):
        right = dev[:, pl.ds(pl.multiple_of(r * Q, Q), Q)]
        for n, i in enumerate(candidates):
            cov = jnp.dot(obs_all[i * Q:(i + 1) * Q, :], right, preferred_element_type=F32)
            for oh in range(2):
                for ch in range(2):
                    factor = table[dense_s[2 * r + ch, 2 * i + oh]]
                    some = cov[oh * BLK:(oh + 1) * BLK, ch * BLK:(ch + 1) * BLK] * factor
                    tapered[n * Q + oh * BLK:n * Q + (oh + 1) * BLK, ch * BLK:(ch + 1) * BLK] = some.astype(BF16)

    def pipelined(cov, change, after):
        cov(0, 0)

        def step(p, carry):
            change(2 * p, 0)
            cov(2 * p + 1, 1)
            change(2 * p + 1, 1)
            cov(2 * p + 2, 0)
            after(p)
            return carry

        lax.fori_loop(0, ROWS // 2 - 1, step, 0)
        change(ROWS - 2, 0)
        cov(ROWS - 1, 1)
        change(ROWS - 1, 1)
        after(ROWS // 2 - 1)

    own = (own0, own1)

    def own_change(r, slot):
        part[r] = jnp.dot(innov_all[:, HALO:HALO + CELLS], own[slot][...], preferred_element_type=F32)

    pipelined(lambda r, slot: covariance(r, range(2, 10), own[slot]), own_change, lambda p: None)

    for copy in innov_halo + obs_halo:
        copy.wait()
    outer = (out0, out1)

    def outer_change(r, slot):
        change = part[r] + jnp.dot(innov_all[:, 0:HALO], outer[slot][0:HALO, :], preferred_element_type=F32)
        change += jnp.dot(innov_all[:, HALO + CELLS:], outer[slot][HALO:, :], preferred_element_type=F32)
        state = region[:, r].astype(F32)
        parts = [
            state[:, h * MD:(h + 1) * MD, :] + change[:, h * BLK:(h + 1) * BLK].reshape(NW, MD, BLK)
            for h in range(2)
        ]
        back[:, r] = jnp.concatenate(parts, axis=1).astype(BF16)

    def send_pair(p):
        rows = pl.ds(2 * p, 2)

        def send_back(other):
            pltpu.make_async_remote_copy(
                src_ref=back.at[other, rows], dst_ref=home.at[me, rows],
                send_sem=b_send, recv_sem=b_recv,
                device_id={"wide": other}, device_id_type=MESH).start()

        def send(k, carry):
            other = chip(k)
            send_back(other)
            send_back(other + 1)
            return carry

        lax.fori_loop(0, len(OFFSETS), send, 0)
        send_back(sibling)
        pltpu.make_async_copy(back.at[me, rows], home.at[me, rows], b_recv).start()

    pipelined(lambda r, slot: covariance(r, (0, 1, 10, 11), outer[slot]), outer_change, send_pair)

    for j, (row0, rows) in enumerate(CHUNKS):
        some = sent.at[pl.ds(0, NW - 1), pl.ds(row0, rows)]
        pltpu.make_async_copy(some, some, a_send.at[j]).wait()
    some = back.at[pl.ds(0, NW - 1)]
    pltpu.make_async_copy(some, some, b_send).wait()
    pltpu.make_async_copy(home, home, b_recv).wait()


def settle(home_ref, out_ref):
    def pair(g, carry):
        v = home_ref[pl.ds(2 * g, 2)].astype(F32)
        for h in range(2):
            u = v[:, :, h * MD:(h + 1) * MD, :]
            parts = [jnp.transpose(u[0], (1, 0, 2)), jnp.transpose(u[1], (1, 0, 2))]
            out_ref[:, pl.ds(pl.multiple_of(g * 16, 16), 16), h * BLK:(h + 1) * BLK] = (
                jnp.concatenate(parts, axis=1).astype(BF16))
        return carry

    lax.fori_loop(0, home_ref.shape[0] // 2, pair, 0, unroll=2)


def body(x, innov, obs_index, obs_weight, obs_list, tile_count, taper_class):
    anywhere = pl.BlockSpec(memory_space=pl.ANY)
    dma = pltpu.SemaphoreType.DMA
    home = pl.pallas_call(
        kernel,
        out_shape=jax.ShapeDtypeStruct((NW, ROWS, 16, BLK), BF16),
        in_specs=[pl.BlockSpec(memory_space=pltpu.HBM)] * 7,
        out_specs=anywhere,
        scratch_shapes=[
            pltpu.VMEM((MD, 256, Q), BF16),
            pltpu.VMEM((MD, 256 + 16, Q), F32),
            pltpu.VMEM((2, 32, BLK), BF16),
            pltpu.VMEM((2, 32, BLK), BF16),
            pltpu.VMEM((2, 32, BLK), F32),
            pltpu.VMEM((NW, ROWS, 16, BLK), BF16),
            pltpu.VMEM((NW, ROWS, 16, BLK), BF16),
            pltpu.VMEM((M, ROWS, Q), BF16),
            pltpu.VMEM((M, CAND), BF16),
            pltpu.VMEM((4, ROWS, Q), jnp.int32),
            pltpu.VMEM((4, ROWS, Q), F32),
            pltpu.VMEM((CELLS, BLK), F32),
            pltpu.VMEM((CELLS, CELLS), BF16),
            pltpu.VMEM((M, CELLS), BF16),
            pltpu.VMEM((CELLS, M), F32),
            pltpu.VMEM((CAND, M), BF16),
            pltpu.VMEM((5, BLK, BLK), F32),
            pltpu.VMEM((1, 16, 16), jnp.int32),
            pltpu.VMEM((1, 16, 16), jnp.int32),
            pltpu.SMEM((1, 16), jnp.int32),
            pltpu.VMEM((16, BLK), jnp.int32),
            pltpu.SMEM((16, BLK), jnp.int32),
            pltpu.VMEM((CELLS, Q), BF16),
            pltpu.VMEM((CELLS, Q), BF16),
            pltpu.VMEM((2 * HALO, Q), BF16),
            pltpu.VMEM((2 * HALO, Q), BF16),
            pltpu.VMEM((ROWS, M, Q), F32),
            pltpu.VMEM((NW, ROWS, 16, BLK), BF16),
            dma((7,)), dma((2,)), dma((2,)), dma((len(CHUNKS),)), dma((len(CHUNKS),)),
            dma((2,)), dma((2,)), dma((2,)), dma((2,)), dma, dma, dma,
        ],
        compiler_params=pltpu.CompilerParams(
            collective_id=0, has_side_effects=True, vmem_limit_bytes=62 * 1024 * 1024),
    )(x, innov, obs_index, obs_weight, obs_list, tile_count, taper_class)
    part = 8
    return pl.pallas_call(
        settle,
        out_shape=jax.ShapeDtypeStruct((MD, 256, Q), BF16),
        grid=(NW // part,),
        in_specs=[pl.BlockSpec((part, ROWS, 16, BLK), lambda i: (i, 0, 0, 0))],
        out_specs=pl.BlockSpec((MD, part * ROWS, Q), lambda i: (0, i, 0)),
    )(home)


def solution(mesh):
    in_specs = (
        P("wide", None, "lon"),
        P(None, "wide", "lon"),
        P(None, None, "lon"),
        P(None, None, "lon"),
        P("lon", "wide", None),
        P("lon", "wide"),
        P("lon", "wide", None),
    )
    return jax.shard_map(
        body, mesh=mesh, in_specs=in_specs, out_specs=P("wide", None, "lon"), check_vma=False)
```

```python
import functools

import jax
import jax.numpy as jnp
from jax import lax
from jax.experimental import pallas as pl
from jax.experimental.pallas import tpu as pltpu
from jax.sharding import PartitionSpec as P

MESH = pl.DeviceIdType.MESH
F32 = jnp.float32
BF16 = jnp.bfloat16

M = 256
ROWS = 8
Q = 256
NW = 32
NL = 8
MD = 8
BLK = 128
HALO = 512
CELLS = ROWS * Q
CAND = CELLS + 2 * HALO
CHUNKS = 2
PAIR = ROWS // CHUNKS
CHIPS = 16
EARLY = 12
GROUP = 64


def iota(shape, dim):
    return lax.broadcasted_iota(jnp.int32, shape, dim)


def kernel(
    x_hbm, innov_hbm, idx_hbm, wgt_hbm, list_hbm, count_hbm, class_hbm, home,
    x_in, x_f, edge_out, edge_in, edge_f, sent, region, innov_in, innov_all, idx, wgt, cols, sel,
    dev, obs_acc, obs_all, table, listed, classes, count_s, dense_v, dense_s,
    own0, own1, out0, out1, part, back,
    load_sem, edge_send, edge_recv, a_send, a_recv, ih_send, ih_recv, oh_send, oh_recv,
    b_send, b_recv, class_sem,
):
    me = lax.axis_index("wide")
    tile = lax.axis_index("lon")
    east = lax.rem(tile + 1, NL)
    west = lax.rem(tile + NL - 1, NL)
    core = lax.rem(me, 2)
    my_x = lax.rem(lax.div(me, 2), 4)
    my_y = lax.div(me, 8)

    def chip(k):
        def offset(i):
            return jnp.where(i == 0, 2, jnp.where(i == 3, 0, 2 * i - 1))

        to_y = lax.rem(my_y + offset(lax.div(k, 4)), 4)
        to_x = lax.rem(my_x + offset(lax.rem(k, 4)), 4)
        return to_y * 8 + to_x * 2

    first = pl.multiple_of(me * ROWS, ROWS)
    loads = [
        pltpu.make_async_copy(src, dst, load_sem.at[i]) for i, (src, dst) in enumerate((
            (x_hbm, x_in),
            (idx_hbm.at[:, pl.ds(first, ROWS), :], idx),
            (wgt_hbm.at[:, pl.ds(first, ROWS), :], wgt),
            (innov_hbm, innov_in),
            (list_hbm, listed),
            (count_hbm, count_s),
            (class_hbm, classes),
        ))
    ]
    load_x, load_idx, load_wgt, load_innov, load_list, load_count, load_class = loads
    for load in loads:
        load.start()

    barrier = pltpu.get_barrier_semaphore()

    def greet(k, carry):
        other = lax.rem(me + k, NW)
        pl.semaphore_signal(barrier, inc=1, device_id={"wide": other}, device_id_type=MESH)
        return carry

    for t in (east, west):
        pl.semaphore_signal(barrier, inc=1, device_id={"lon": t}, device_id_type=MESH)
    lax.fori_loop(1, NW, greet, 0)

    x_f[0] = jnp.zeros((MD, Q), F32)
    x_f[257] = jnp.zeros((MD, Q), F32)
    load_x.wait()

    def widen(g, carry):
        r0 = pl.multiple_of(g * 16, 16)
        v = x_in[:, pl.ds(r0, 16), :].astype(F32)
        lane = iota((MD, BLK), 1)
        firsts = jnp.zeros((MD, BLK), F32)
        lasts = jnp.zeros((MD, BLK), F32)
        for i in range(0, 16, 8):
            a = jnp.transpose(v[:, i:i + 8, :BLK], (1, 0, 2))
            b = jnp.transpose(v[:, i:i + 8, BLK:], (1, 0, 2))
            x_f[pl.ds(r0 + i + 1, 8)] = jnp.concatenate([a, b], axis=2)
            for j in range(8):
                k = i + j
                firsts = jnp.where(lane == k, pltpu.roll(a[j], k, 1) if k else a[j], firsts)
                lasts = jnp.where(lane == k, pltpu.roll(b[j], k + 1, 1), lasts)
        turns = lax.rem(g, 8) * 16
        wide_lane = iota((MD, Q), 1) - r0
        here = (wide_lane >= 0) & (wide_lane < 16)

        def place(new, old):
            new = pltpu.roll(new, turns, 1)
            return jnp.where(here, jnp.concatenate([new, new], axis=1), old)

        return place(firsts, carry[0]), place(lasts, carry[1])

    zeros = jnp.zeros((MD, Q), F32)
    left, right = lax.fori_loop(0, 16, widen, (zeros, zeros), unroll=2)
    edge_out[0] = jnp.concatenate([left, zeros], axis=0).astype(BF16)
    edge_out[1] = jnp.concatenate([right, zeros], axis=0).astype(BF16)

    d = (iota((BLK, BLK), 0) - iota((BLK, BLK), 1)).astype(F32)
    for c in range(4):
        s = d * (1.0 / (8.0 * 2.0 ** c))
        table[c] = (1.0 / (M - 1.0)) / (1.0 + s * s)
    table[4] = jnp.zeros((BLK, BLK), F32)

    load_idx.wait()
    load_wgt.wait()
    origin = me * CELLS

    def columns(i, carry):
        parts = [(idx[k, pl.ds(i, 1), :] - origin).astype(F32) for k in range(4)]
        parts += [wgt[k, pl.ds(i, 1), :] for k in range(4)]
        stacked = jnp.concatenate(parts + [jnp.zeros((BLK - 8, Q), F32)], axis=0)
        cols[pl.ds(pl.multiple_of(i * Q, Q), Q), :] = jnp.transpose(stacked, (1, 0))
        return carry

    lax.fori_loop(0, ROWS, columns, 0, unroll=2)

    pl.semaphore_wait(barrier, NW - 1 + 2)

    def lon_copy(src, dst, send_sem, recv_sem, t):
        copy = pltpu.make_async_remote_copy(
            src_ref=src, dst_ref=dst, send_sem=send_sem, recv_sem=recv_sem,
            device_id={"lon": t}, device_id_type=MESH)
        copy.start()
        return copy

    edges = [
        lon_copy(edge_out.at[side], edge_in.at[side], edge_send.at[side], edge_recv.at[side], t)
        for side, t in ((0, west), (1, east))
    ]

    load_innov.wait()

    def turn(g, carry):
        m0 = pl.multiple_of(g * 16, 16)
        v = innov_in[pl.ds(m0, 16)].astype(F32)
        parts = [jnp.transpose(v[:8], (1, 0, 2)), jnp.transpose(v[8:], (1, 0, 2))]
        u = jnp.concatenate(parts, axis=1).astype(BF16)
        for r in range(ROWS):
            innov_all[pl.ds(m0, 16), HALO + r * Q:HALO + (r + 1) * Q] = u[r]
        return carry

    lax.fori_loop(0, M // 16, turn, 0)
    innov_halo = [
        lon_copy(innov_all.at[:, pl.ds(CELLS, HALO)], innov_all.at[:, pl.ds(0, HALO)],
                 ih_send.at[0], ih_recv.at[0], east),
        lon_copy(innov_all.at[:, pl.ds(HALO, HALO)], innov_all.at[:, pl.ds(HALO + CELLS, HALO)],
                 ih_send.at[1], ih_recv.at[1], west),
    ]

    for load in (load_list, load_count, load_class):
        load.wait()
    block = iota((16, BLK), 0)
    ids = iota((16, BLK), 1)
    counts = jnp.zeros((16, BLK), jnp.int32)
    for b in range(16):
        counts = jnp.where(block == b, count_s[0, b], counts)
    dense = jnp.full((16, BLK), 4, jnp.int32)
    for j in range(16):
        hit = (ids == listed[0, :, j:j + 1]) & (counts > j)
        dense = jnp.where(hit, classes[0, :, j:j + 1], dense)
    dense_v[...] = dense
    to_scalar = pltpu.make_async_copy(dense_v, dense_s, class_sem)
    to_scalar.start()

    def select(g, carry):
        o0 = pl.multiple_of(g * GROUP, GROUP)
        here = cols[pl.ds(o0, GROUP), :]
        cell = [jnp.broadcast_to(here[:, k:k + 1], (GROUP, BLK)) for k in range(4)]
        cell = [c.astype(jnp.int32).astype(jnp.int16) for c in cell]
        weight = [jnp.broadcast_to(here[:, 4 + k:5 + k], (GROUP, BLK)).astype(BF16) for k in range(4)]
        none = jnp.zeros((GROUP, BLK), BF16)
        sums = []
        for k in range(4):
            total = weight[k]
            for j in range(k):
                total = total + jnp.where(cell[j] == cell[k], weight[j], none)
            sums.append(total)
        lanes = iota((GROUP, BLK), 1).astype(jnp.int16)
        for t in range(CELLS // BLK):
            at = lanes + jnp.int16(t * BLK)
            value = jnp.where(at == cell[0], sums[0], none)
            for k in range(1, 4):
                value = jnp.where(at == cell[k], sums[k], value)
            sel[pl.ds(o0, GROUP), t * BLK:(t + 1) * BLK] = value
        return carry

    steps = CELLS // GROUP
    lax.fori_loop(0, EARLY, select, 0, unroll=2)

    for copy in edges:
        copy.wait()
    for side in range(2):
        got = edge_in[side].astype(F32)
        for h in range(2):
            edge_f[side, h] = got[:MD, h * BLK:(h + 1) * BLK]

    def forecast(r):
        lane = iota((MD, BLK), 1)
        turns = lax.rem(BLK - lax.rem(r, 16) * 8, BLK)
        e_in = pltpu.roll(edge_f[0, lax.div(r, 16)], turns, 1)
        w_in = pltpu.roll(edge_f[1, lax.div(r, 16)], turns, 1)
        for i in range(ROWS):
            at = r * ROWS + i
            s, v, n = x_f[at], x_f[at + 1], x_f[at + 2]
            a, b = v[:, :BLK], v[:, BLK:]
            a_up, b_up = pltpu.roll(a, BLK - 1, 1), pltpu.roll(b, BLK - 1, 1)
            a_dn, b_dn = pltpu.roll(a, 1, 1), pltpu.roll(b, 1, 1)
            e_edge = pltpu.roll(e_in, BLK - 1 - i, 1)
            w_edge = pltpu.roll(w_in, BLK - i, 1) if i else w_in
            e_a = jnp.where(lane == BLK - 1, b_up, a_up)
            e_b = jnp.where(lane == BLK - 1, e_edge, b_up)
            w_a = jnp.where(lane == 0, w_edge, a_dn)
            w_b = jnp.where(lane == 0, a_dn, b_dn)
            halves = []
            for h, (c, e, w) in enumerate(((a, e_a, w_a), (b, e_b, w_b))):
                hs = slice(h * BLK, (h + 1) * BLK)
                spread = e + w + n[:, hs] + s[:, hs] - 4.0 * c
                halves.append(c + 0.2 * spread - 0.3 * (e - w))
            sent[r, i] = jnp.concatenate(halves, axis=0).astype(BF16)

    def send_forecast(other, j):
        rows = pl.ds(j * PAIR, PAIR)

        @pl.when(other == me)
        def _():
            pltpu.make_async_copy(sent.at[me, rows], region.at[me, rows], a_recv.at[j]).start()

        @pl.when(other != me)
        def _():
            pltpu.make_async_remote_copy(
                src_ref=sent.at[other, rows], dst_ref=region.at[me, rows],
                send_sem=a_send.at[j], recv_sem=a_recv.at[j],
                device_id={"wide": other}, device_id_type=MESH).start()

    def phase(c, carry):
        def compute_send(p, inner):
            others = [chip(2 * p) + c, chip(2 * p + 1) + c]
            for other in others:
                forecast(other)
            for other in others:
                send_forecast(other, 0)
            return inner

        lax.fori_loop(0, CHIPS // 2, compute_send, 0)

        def send_rest(k, inner):
            for j in range(1, CHUNKS):
                send_forecast(chip(k) + c, j)
            return inner

        lax.fori_loop(0, CHIPS, send_rest, 0)
        return carry

    lax.fori_loop(0, 2, phase, 0)

    lax.fori_loop(EARLY, steps, select, 0, unroll=2)

    def anomaly(r, carry):
        v = region[:, r].astype(F32)
        for h in range(2):
            u = v[:, h * MD:(h + 1) * MD, :].reshape(M, BLK)
            u = u - jnp.sum(u, axis=0, keepdims=True) * (1.0 / M)
            dev[:, pl.ds(pl.multiple_of(r * Q + h * BLK, BLK), BLK)] = u.astype(BF16)
        return carry

    def lon_plan(src, dst, send_sem, recv_sem, t):
        return pltpu.make_async_remote_copy(
            src_ref=src, dst_ref=dst, send_sem=send_sem, recv_sem=recv_sem,
            device_id={"lon": t}, device_id_type=MESH)

    obs_halo = [
        lon_plan(obs_all.at[pl.ds(CELLS, HALO)], obs_all.at[pl.ds(0, HALO)],
                 oh_send.at[0], oh_recv.at[0], east),
        lon_plan(obs_all.at[pl.ds(HALO, HALO)], obs_all.at[pl.ds(HALO + CELLS, HALO)],
                 oh_send.at[1], oh_recv.at[1], west),
    ]
    obs_acc[...] = jnp.zeros((CELLS, M), F32)

    def observe(j, carry):
        arrived = region.at[:, pl.ds(j * PAIR, PAIR)]
        pltpu.make_async_copy(arrived, arrived, a_recv.at[j]).wait()
        lax.fori_loop(0, PAIR, lambda i, inner: anomaly(j * PAIR + i, inner), 0, unroll=2)
        cells = pl.ds(pl.multiple_of(j * PAIR * Q, Q), PAIR * Q)

        def product(k, inner):
            o = jnp.where(k == 1, 3, jnp.where(k > 1, k - 1, 0))
            at = pl.ds(pl.multiple_of(o * HALO, HALO), HALO)
            total = obs_acc[at, :] + lax.dot_general(
                sel[at, cells], dev[:, cells], (((1,), (1,)), ((), ())), preferred_element_type=F32)
            obs_acc[at, :] = total
            obs_all[pl.ds(pl.multiple_of(o * HALO + HALO, HALO), HALO), :] = total.astype(BF16)
            return inner

        lax.fori_loop(0, 2, product, 0)

        @pl.when(j == CHUNKS - 1)
        def _():
            for copy in obs_halo:
                copy.start()

        lax.fori_loop(2, CELLS // HALO, product, 0)
        return carry

    lax.fori_loop(0, CHUNKS, observe, 0)

    to_scalar.wait()

    def covariance(r, candidates, tapered):
        right = dev[:, pl.ds(r * Q if isinstance(r, int) else pl.multiple_of(r * Q, Q), Q)]
        for n, i in enumerate(candidates):
            cov = jnp.dot(obs_all[i * Q:(i + 1) * Q, :], right, preferred_element_type=F32)
            for oh in range(2):
                for ch in range(2):
                    factor = table[dense_s[2 * r + ch, 2 * i + oh]]
                    some = cov[oh * BLK:(oh + 1) * BLK, ch * BLK:(ch + 1) * BLK] * factor
                    tapered[n * Q + oh * BLK:n * Q + (oh + 1) * BLK, ch * BLK:(ch + 1) * BLK] = some.astype(BF16)

    def pipelined(cov, change, after):
        cov(0, 0)

        def step(p, carry):
            change(2 * p, 0)
            cov(2 * p + 1, 1)
            change(2 * p + 1, 1)
            cov(jnp.minimum(2 * p + 2, ROWS - 1), 0)
            after(p)
            return carry

        lax.fori_loop(0, ROWS // 2, step, 0)

    own = (own0, own1)

    def own_change(r, slot):
        part[r] = jnp.dot(innov_all[:, HALO:HALO + CELLS], own[slot][...], preferred_element_type=F32)

    pipelined(lambda r, slot: covariance(r, range(2, 10), own[slot]), own_change, lambda p: None)

    for copy in innov_halo + obs_halo:
        copy.wait()
    outer = (out0, out1)

    def outer_change(r, slot):
        change = part[r] + jnp.dot(innov_all[:, 0:HALO], outer[slot][0:HALO, :], preferred_element_type=F32)
        change += jnp.dot(innov_all[:, HALO + CELLS:], outer[slot][HALO:, :], preferred_element_type=F32)
        state = region[:, r].astype(F32)
        parts = [
            state[:, h * MD:(h + 1) * MD, :] + change[:, h * BLK:(h + 1) * BLK].reshape(NW, MD, BLK)
            for h in range(2)
        ]
        back[:, r] = jnp.concatenate(parts, axis=1).astype(BF16)

    chip_columns = [lax.rem(my_x + offset, 4) * 2 for offset in (2, 1, 3, 0)]
    sibling = lax.div(me, 2) * 2 + 1 - core

    def send_pair(p):
        rows = pl.ds(2 * p, 2)

        def send_back(other):
            pltpu.make_async_remote_copy(
                src_ref=back.at[other, rows], dst_ref=home.at[me, rows],
                send_sem=b_send, recv_sem=b_recv,
                device_id={"wide": other}, device_id_type=MESH).start()

        def send(k, carry):
            to_row = lax.rem(my_y + jnp.where(k == 0, 2, 2 * k - 1), 4) * 8
            for column in chip_columns:
                send_back(to_row + column)
                send_back(to_row + column + 1)
            return carry

        lax.fori_loop(0, 3, send, 0)
        for column in chip_columns[:3]:
            send_back(my_y * 8 + column)
            send_back(my_y * 8 + column + 1)
        send_back(sibling)
        pltpu.make_async_copy(back.at[me, rows], home.at[me, rows], b_recv).start()

    pipelined(lambda r, slot: covariance(r, (0, 1, 10, 11), outer[slot]), outer_change, send_pair)

    for j in range(CHUNKS):
        some = sent.at[pl.ds(0, NW - 1), pl.ds(j * PAIR, PAIR)]
        pltpu.make_async_copy(some, some, a_send.at[j]).wait()
    some = back.at[pl.ds(0, NW - 1)]
    pltpu.make_async_copy(some, some, b_send).wait()
    pltpu.make_async_copy(home, home, b_recv).wait()


def settle(home_ref, out_ref):
    def pair(g, carry):
        v = home_ref[pl.ds(2 * g, 2)].astype(F32)
        for h in range(2):
            u = v[:, :, h * MD:(h + 1) * MD, :]
            parts = [jnp.transpose(u[0], (1, 0, 2)), jnp.transpose(u[1], (1, 0, 2))]
            out_ref[:, pl.ds(pl.multiple_of(g * 16, 16), 16), h * BLK:(h + 1) * BLK] = (
                jnp.concatenate(parts, axis=1).astype(BF16))
        return carry

    lax.fori_loop(0, home_ref.shape[0] // 2, pair, 0, unroll=2)


def body(x, innov, obs_index, obs_weight, obs_list, tile_count, taper_class):
    anywhere = pl.BlockSpec(memory_space=pl.ANY)
    dma = pltpu.SemaphoreType.DMA
    home = pl.pallas_call(
        kernel,
        out_shape=jax.ShapeDtypeStruct((NW, ROWS, 16, BLK), BF16),
        in_specs=[pl.BlockSpec(memory_space=pltpu.HBM)] * 7,
        out_specs=anywhere,
        scratch_shapes=[
            pltpu.VMEM((MD, 256, Q), BF16),
            pltpu.VMEM((256 + 2, MD, Q), F32),
            pltpu.VMEM((2, 16, Q), BF16),
            pltpu.VMEM((2, 16, Q), BF16),
            pltpu.VMEM((2, 2, MD, BLK), F32),
            pltpu.VMEM((NW, ROWS, 16, BLK), BF16),
            pltpu.VMEM((NW, ROWS, 16, BLK), BF16),
            pltpu.VMEM((M, ROWS, Q), BF16),
            pltpu.VMEM((M, CAND), BF16),
            pltpu.VMEM((4, ROWS, Q), jnp.int32),
            pltpu.VMEM((4, ROWS, Q), F32),
            pltpu.VMEM((CELLS, BLK), F32),
            pltpu.VMEM((CELLS, CELLS), BF16),
            pltpu.VMEM((M, CELLS), BF16),
            pltpu.VMEM((CELLS, M), F32),
            pltpu.VMEM((CAND, M), BF16),
            pltpu.VMEM((5, BLK, BLK), F32),
            pltpu.VMEM((1, 16, 16), jnp.int32),
            pltpu.VMEM((1, 16, 16), jnp.int32),
            pltpu.SMEM((1, 16), jnp.int32),
            pltpu.VMEM((16, BLK), jnp.int32),
            pltpu.SMEM((16, BLK), jnp.int32),
            pltpu.VMEM((CELLS, Q), BF16),
            pltpu.VMEM((CELLS, Q), BF16),
            pltpu.VMEM((2 * HALO, Q), BF16),
            pltpu.VMEM((2 * HALO, Q), BF16),
            pltpu.VMEM((ROWS, M, Q), F32),
            pltpu.VMEM((NW, ROWS, 16, BLK), BF16),
            dma((7,)), dma((2,)), dma((2,)), dma((CHUNKS,)), dma((CHUNKS,)),
            dma((2,)), dma((2,)), dma((2,)), dma((2,)), dma, dma, dma,
        ],
        compiler_params=pltpu.CompilerParams(
            collective_id=0, has_side_effects=True, vmem_limit_bytes=62 * 1024 * 1024),
    )(x, innov, obs_index, obs_weight, obs_list, tile_count, taper_class)
    part = NW // 2
    return pl.pallas_call(
        settle,
        out_shape=jax.ShapeDtypeStruct((MD, 256, Q), BF16),
        grid=(NW // part,),
        in_specs=[pl.BlockSpec((part, ROWS, 16, BLK), lambda i: (i, 0, 0, 0))],
        out_specs=pl.BlockSpec((MD, part * ROWS, Q), lambda i: (0, i, 0)),
    )(home)


def solution(mesh):
    in_specs = (
        P("wide", None, "lon"),
        P(None, "wide", "lon"),
        P(None, None, "lon"),
        P(None, None, "lon"),
        P("lon", "wide", None),
        P("lon", "wide"),
        P("lon", "wide", None),
    )
    return jax.shard_map(
        body, mesh=mesh, in_specs=in_specs, out_specs=P("wide", None, "lon"), check_vma=False)
```

```python
import functools

import jax
import jax.numpy as jnp
from jax import lax
from jax.experimental import pallas as pl
from jax.experimental.pallas import tpu as pltpu
from jax.sharding import PartitionSpec as P

MESH = pl.DeviceIdType.MESH
F32 = jnp.float32
BF16 = jnp.bfloat16

M = 256
ROWS = 8
Q = 256
NW = 32
NL = 8
MD = 8
BLK = 128
HALO = 512
CELLS = ROWS * Q
CAND = CELLS + 2 * HALO
CHUNKS = 2
PAIR = ROWS // CHUNKS
PARTS = 4
HALF = 4
CHIPS = 16
STEP = 2
EARLY = 6
GROUP = 64


def iota(shape, dim):
    return lax.broadcasted_iota(jnp.int32, shape, dim)


def kernel(
    x_hbm, innov_hbm, idx_hbm, wgt_hbm, list_hbm, count_hbm, class_hbm, home,
    x_in, x_f, edge_out, edge_in, edge_f, sent, region, innov_in, innov_all, idx, wgt, cols, sel,
    dev, obs_acc, obs_all, table, listed, classes, count_s, dense_v, dense_s,
    own0, own1, out0, out1, part, back,
    x_sem, load_sem, edge_send, edge_recv, a_send, a_recv, ih_send, ih_recv, oh_send, oh_recv,
    b_send, b_recv, class_sem,
):
    me = lax.axis_index("wide")
    tile = lax.axis_index("lon")
    east = lax.rem(tile + 1, NL)
    west = lax.rem(tile + NL - 1, NL)
    core = lax.rem(me, 2)
    my_x = lax.rem(lax.div(me, 2), 4)
    my_y = lax.div(me, 8)

    def chip(k):
        def offset(i):
            return jnp.where(i == 0, 2, jnp.where(i == 3, 0, 2 * i - 1))

        to_y = lax.rem(my_y + offset(lax.div(k, 4)), 4)
        to_x = lax.rem(my_x + offset(lax.rem(k, 4)), 4)
        return to_y * 8 + to_x * 2

    first = pl.multiple_of(me * ROWS, ROWS)
    loads = [
        pltpu.make_async_copy(src, dst, load_sem.at[i]) for i, (src, dst) in enumerate((
            (idx_hbm.at[:, pl.ds(first, ROWS), :], idx),
            (wgt_hbm.at[:, pl.ds(first, ROWS), :], wgt),
            (innov_hbm, innov_in),
            (list_hbm, listed),
            (count_hbm, count_s),
            (class_hbm, classes),
        ))
    ]
    load_idx, load_wgt, load_innov, load_list, load_count, load_class = loads
    load_x = pltpu.make_async_copy(x_hbm, x_in, x_sem)
    load_x.start()

    barrier = pltpu.get_barrier_semaphore()

    def greet(k, carry):
        other = lax.rem(me + k, NW)
        pl.semaphore_signal(barrier, inc=1, device_id={"wide": other}, device_id_type=MESH)
        return carry

    for t in (east, west):
        pl.semaphore_signal(barrier, inc=1, device_id={"lon": t}, device_id_type=MESH)
    lax.fori_loop(1, NW, greet, 0)

    x_f[0] = jnp.zeros((MD, Q), F32)
    x_f[257] = jnp.zeros((MD, Q), F32)
    load_x.wait()
    for load in loads:
        load.start()

    def widen(g, carry):
        r0 = pl.multiple_of(g * 16, 16)
        v = x_in[:, pl.ds(r0, 16), :].astype(F32)
        lane = iota((MD, BLK), 1)
        firsts = jnp.zeros((MD, BLK), F32)
        lasts = jnp.zeros((MD, BLK), F32)
        for i in range(0, 16, 8):
            a = jnp.transpose(v[:, i:i + 8, :BLK], (1, 0, 2))
            b = jnp.transpose(v[:, i:i + 8, BLK:], (1, 0, 2))
            x_f[pl.ds(r0 + i + 1, 8)] = jnp.concatenate([a, b], axis=2)
            for j in range(8):
                k = i + j
                firsts = jnp.where(lane == k, pltpu.roll(a[j], k, 1) if k else a[j], firsts)
                lasts = jnp.where(lane == k, pltpu.roll(b[j], k + 1, 1), lasts)
        turns = lax.rem(g, 8) * 16
        wide_lane = iota((MD, Q), 1) - r0
        here = (wide_lane >= 0) & (wide_lane < 16)

        def place(new, old):
            new = pltpu.roll(new, turns, 1)
            return jnp.where(here, jnp.concatenate([new, new], axis=1), old)

        return place(firsts, carry[0]), place(lasts, carry[1])

    zeros = jnp.zeros((MD, Q), F32)
    left, right = lax.fori_loop(0, 16, widen, (zeros, zeros), unroll=4)
    edge_out[0] = jnp.concatenate([left, zeros], axis=0).astype(BF16)
    edge_out[1] = jnp.concatenate([right, zeros], axis=0).astype(BF16)

    pl.semaphore_wait(barrier, NW - 1 + 2)

    def lon_copy(src, dst, send_sem, recv_sem, t):
        copy = pltpu.make_async_remote_copy(
            src_ref=src, dst_ref=dst, send_sem=send_sem, recv_sem=recv_sem,
            device_id={"lon": t}, device_id_type=MESH)
        copy.start()
        return copy

    edges = [
        lon_copy(edge_out.at[side], edge_in.at[side], edge_send.at[side], edge_recv.at[side], t)
        for side, t in ((0, west), (1, east))
    ]

    load_idx.wait()
    load_wgt.wait()
    origin = me * CELLS

    def columns(i, carry):
        parts = [(idx[k, pl.ds(i, 1), :] - origin).astype(F32) for k in range(4)]
        parts += [wgt[k, pl.ds(i, 1), :] for k in range(4)]
        stacked = jnp.concatenate(parts + [jnp.zeros((BLK - 8, Q), F32)], axis=0)
        cols[pl.ds(pl.multiple_of(i * Q, Q), Q), :] = jnp.transpose(stacked, (1, 0))
        return carry

    lax.fori_loop(0, ROWS, columns, 0, unroll=2)

    load_innov.wait()

    def turn(g, carry):
        m0 = pl.multiple_of(g * 16, 16)
        v = innov_in[pl.ds(m0, 16)].astype(F32)
        parts = [jnp.transpose(v[:8], (1, 0, 2)), jnp.transpose(v[8:], (1, 0, 2))]
        u = jnp.concatenate(parts, axis=1).astype(BF16)
        for r in range(ROWS):
            innov_all[pl.ds(m0, 16), HALO + r * Q:HALO + (r + 1) * Q] = u[r]
        return carry

    lax.fori_loop(0, M // 16, turn, 0)
    innov_halo = [
        lon_copy(innov_all.at[:, pl.ds(CELLS, HALO)], innov_all.at[:, pl.ds(0, HALO)],
                 ih_send.at[0], ih_recv.at[0], east),
        lon_copy(innov_all.at[:, pl.ds(HALO, HALO)], innov_all.at[:, pl.ds(HALO + CELLS, HALO)],
                 ih_send.at[1], ih_recv.at[1], west),
    ]

    d = (iota((BLK, BLK), 0) - iota((BLK, BLK), 1)).astype(F32)
    for c in range(4):
        s = d * (1.0 / (8.0 * 2.0 ** c))
        table[c] = (1.0 / (M - 1.0)) / (1.0 + s * s)
    table[4] = jnp.zeros((BLK, BLK), F32)

    for load in (load_list, load_count, load_class):
        load.wait()
    block = iota((16, BLK), 0)
    ids = iota((16, BLK), 1)
    counts = jnp.zeros((16, BLK), jnp.int32)
    for b in range(16):
        counts = jnp.where(block == b, count_s[0, b], counts)
    dense = jnp.full((16, BLK), 4, jnp.int32)
    for j in range(16):
        hit = (ids == listed[0, :, j:j + 1]) & (counts > j)
        dense = jnp.where(hit, classes[0, :, j:j + 1], dense)
    dense_v[...] = dense
    to_scalar = pltpu.make_async_copy(dense_v, dense_s, class_sem)
    to_scalar.start()

    def select(g, carry):
        o0 = pl.multiple_of(g * GROUP, GROUP)
        to = pl.multiple_of(lax.rem(o0 + HALO, CELLS), GROUP)
        here = cols[pl.ds(o0, GROUP), :]
        cell = [jnp.broadcast_to(here[:, k:k + 1], (GROUP, BLK)) for k in range(4)]
        cell = [c.astype(jnp.int32).astype(jnp.int16) for c in cell]
        weight = [jnp.broadcast_to(here[:, 4 + k:5 + k], (GROUP, BLK)).astype(BF16) for k in range(4)]
        none = jnp.zeros((GROUP, BLK), BF16)
        sums = []
        for k in range(4):
            total = weight[k]
            for j in range(k):
                total = total + jnp.where(cell[j] == cell[k], weight[j], none)
            sums.append(total)
        lanes = iota((GROUP, BLK), 1).astype(jnp.int16)
        for t in range(CELLS // BLK):
            at = lanes + jnp.int16(t * BLK)
            value = jnp.where(at == cell[0], sums[0], none)
            for k in range(1, 4):
                value = jnp.where(at == cell[k], sums[k], value)
            sel[pl.ds(to, GROUP), t * BLK:(t + 1) * BLK] = value
        return carry

    steps = CELLS // GROUP
    lax.fori_loop(0, EARLY, select, 0, unroll=2)

    for copy in edges:
        copy.wait()
    for side in range(2):
        got = edge_in[side].astype(F32)
        for h in range(2):
            edge_f[side, h] = got[:MD, h * BLK:(h + 1) * BLK]

    def forecast(r):
        lane = iota((MD, BLK), 1)
        turns = lax.rem(BLK - lax.rem(r, 16) * 8, BLK)
        e_in = pltpu.roll(edge_f[0, lax.div(r, 16)], turns, 1)
        w_in = pltpu.roll(edge_f[1, lax.div(r, 16)], turns, 1)
        for i in range(ROWS):
            at = r * ROWS + i
            s, v, n = x_f[at], x_f[at + 1], x_f[at + 2]
            a, b = v[:, :BLK], v[:, BLK:]
            a_up, b_up = pltpu.roll(a, BLK - 1, 1), pltpu.roll(b, BLK - 1, 1)
            a_dn, b_dn = pltpu.roll(a, 1, 1), pltpu.roll(b, 1, 1)
            e_edge = pltpu.roll(e_in, BLK - 1 - i, 1)
            w_edge = pltpu.roll(w_in, BLK - i, 1) if i else w_in
            e_a = jnp.where(lane == BLK - 1, b_up, a_up)
            e_b = jnp.where(lane == BLK - 1, e_edge, b_up)
            w_a = jnp.where(lane == 0, w_edge, a_dn)
            w_b = jnp.where(lane == 0, a_dn, b_dn)
            halves = []
            for h, (c, e, w) in enumerate(((a, e_a, w_a), (b, e_b, w_b))):
                hs = slice(h * BLK, (h + 1) * BLK)
                spread = e + w + n[:, hs] + s[:, hs] - 4.0 * c
                halves.append(c + 0.2 * spread - 0.3 * (e - w))
            sent[r, i] = jnp.concatenate(halves, axis=0).astype(BF16)

    def send_forecast(other, j):
        rows = pl.ds(j * PAIR, PAIR)

        @pl.when(other == me)
        def _():
            pltpu.make_async_copy(sent.at[me, rows], region.at[me, rows], a_recv.at[j]).start()

        @pl.when(other != me)
        def _():
            pltpu.make_async_remote_copy(
                src_ref=sent.at[other, rows], dst_ref=region.at[me, rows],
                send_sem=a_send.at[j], recv_sem=a_recv.at[j],
                device_id={"wide": other}, device_id_type=MESH).start()

    def phase(c, carry):
        def compute_send(p, inner):
            others = [chip(STEP * p + i) + c for i in range(STEP)]
            for other in others:
                forecast(other)
            for other in others:
                send_forecast(other, 0)
            return inner

        lax.fori_loop(0, CHIPS // STEP, compute_send, 0)

        def send_rest(k, inner):
            for j in range(1, CHUNKS):
                send_forecast(chip(k) + c, j)
            return inner

        lax.fori_loop(0, CHIPS, send_rest, 0, unroll=4)
        return carry

    lax.fori_loop(0, 2, phase, 0)

    lax.fori_loop(EARLY, steps, select, 0, unroll=2)

    def anomaly(r, carry):
        v = region[:, r].astype(F32)
        for h in range(2):
            u = v[:, h * MD:(h + 1) * MD, :].reshape(M, BLK)
            u = u - jnp.sum(u, axis=0, keepdims=True) * (1.0 / M)
            dev[:, pl.ds(pl.multiple_of(r * Q + h * BLK, BLK), BLK)] = u.astype(BF16)
        return carry

    def lon_plan(src, dst, send_sem, recv_sem, t):
        return pltpu.make_async_remote_copy(
            src_ref=src, dst_ref=dst, send_sem=send_sem, recv_sem=recv_sem,
            device_id={"lon": t}, device_id_type=MESH)

    obs_halo = [
        lon_plan(obs_all.at[pl.ds(CELLS, HALO)], obs_all.at[pl.ds(0, HALO)],
                 oh_send.at[0], oh_recv.at[0], east),
        lon_plan(obs_all.at[pl.ds(HALO, HALO)], obs_all.at[pl.ds(HALO + CELLS, HALO)],
                 oh_send.at[1], oh_recv.at[1], west),
    ]
    obs_acc[...] = jnp.zeros((CELLS, M), F32)

    def product(block, j):
        at = pl.ds(pl.multiple_of(block * 2 * HALO, 2 * HALO), 2 * HALO)
        cells = pl.ds(pl.multiple_of(j * PAIR * Q, Q), PAIR * Q)
        total = obs_acc[at, :] + lax.dot_general(
            sel[at, cells], dev[:, cells], (((1,), (1,)), ((), ())), preferred_element_type=F32)
        obs_acc[at, :] = total
        some = total.astype(BF16)
        to = pl.multiple_of(jnp.where(block == 0, CELLS, 2 * HALO), HALO)
        obs_all[pl.ds(to, HALO), :] = some[:HALO]
        to = pl.multiple_of(jnp.where(block == 0, HALO, 3 * HALO), HALO)
        obs_all[pl.ds(to, HALO), :] = some[HALO:]

    def observe(step, carry):
        block = lax.div(step, CHUNKS)
        j = lax.rem(step, CHUNKS)

        @pl.when(block == 0)
        def _():
            arrived = region.at[:, pl.ds(j * PAIR, PAIR)]
            pltpu.make_async_copy(arrived, arrived, a_recv.at[j]).wait()
            lax.fori_loop(0, PAIR, lambda i, inner: anomaly(j * PAIR + i, inner), 0, unroll=2)

        product(block, j)

        @pl.when(step == CHUNKS - 1)
        def _():
            for copy in obs_halo:
                copy.start()

        return carry

    lax.fori_loop(0, 2 * CHUNKS, observe, 0)

    to_scalar.wait()

    def covariance(r, candidates, tapered):
        right = dev[:, pl.ds(r * Q if isinstance(r, int) else pl.multiple_of(r * Q, Q), Q)]
        for n, i in enumerate(candidates):
            cov = jnp.dot(obs_all[i * Q:(i + 1) * Q, :], right, preferred_element_type=F32)
            for oh in range(2):
                for ch in range(2):
                    factor = table[dense_s[2 * r + ch, 2 * i + oh]]
                    some = cov[oh * BLK:(oh + 1) * BLK, ch * BLK:(ch + 1) * BLK] * factor
                    tapered[n * Q + oh * BLK:n * Q + (oh + 1) * BLK, ch * BLK:(ch + 1) * BLK] = some.astype(BF16)

    def pipelined(base, cov, change, after):
        def step(p, carry):
            r = base + 2 * p
            change(r, 0)
            cov(r + 1, 1)
            change(r + 1, 1)
            cov(jnp.minimum(r + 2, ROWS - 1), 0)
            after(r)
            return carry

        lax.fori_loop(0, HALF // 2, step, 0)

    own = (own0, own1)

    def own_change(r, slot):
        part[r] = jnp.dot(innov_all[:, HALO:HALO + CELLS], own[slot][...], preferred_element_type=F32)

    outer = (out0, out1)

    def outer_change(r, slot):
        change = part[r] + jnp.dot(innov_all[:, 0:HALO], outer[slot][0:HALO, :], preferred_element_type=F32)
        change += jnp.dot(innov_all[:, HALO + CELLS:], outer[slot][HALO:, :], preferred_element_type=F32)
        state = region[:, r].astype(F32)
        parts = [
            state[:, h * MD:(h + 1) * MD, :] + change[:, h * BLK:(h + 1) * BLK].reshape(NW, MD, BLK)
            for h in range(2)
        ]
        back[:, r] = jnp.concatenate(parts, axis=1).astype(BF16)

    chip_columns = [lax.rem(my_x + offset, 4) * 2 for offset in (2, 1, 3, 0)]
    sibling = lax.div(me, 2) * 2 + 1 - core

    def send_pair(r):
        rows = pl.ds(r, 2)

        def send_back(other):
            pltpu.make_async_remote_copy(
                src_ref=back.at[other, rows], dst_ref=home.at[me, rows],
                send_sem=b_send, recv_sem=b_recv,
                device_id={"wide": other}, device_id_type=MESH).start()

        def send(k, carry):
            to_row = lax.rem(my_y + jnp.where(k == 0, 2, 2 * k - 1), 4) * 8
            for column in chip_columns:
                send_back(to_row + column)
                send_back(to_row + column + 1)
            return carry

        lax.fori_loop(0, 3, send, 0)
        for column in chip_columns[:3]:
            send_back(my_y * 8 + column)
            send_back(my_y * 8 + column + 1)
        send_back(sibling)
        pltpu.make_async_copy(back.at[me, rows], home.at[me, rows], b_recv).start()

    def own_covariance(r, slot):
        covariance(r, range(2, 10), own[slot])

    def outer_covariance(r, slot):
        covariance(r, (0, 1, 10, 11), outer[slot])

    own_covariance(0, 0)

    def update(half, carry):
        base = half * HALF
        pipelined(base, own_covariance, own_change, lambda r: None)

        @pl.when(half == 0)
        def _():
            for copy in innov_halo + obs_halo:
                copy.wait()
            outer_covariance(0, 0)

        pipelined(base, outer_covariance, outer_change, send_pair)
        return carry

    lax.fori_loop(0, ROWS // HALF, update, 0)

    for j in range(CHUNKS):
        some = sent.at[pl.ds(0, NW - 1), pl.ds(j * PAIR, PAIR)]
        pltpu.make_async_copy(some, some, a_send.at[j]).wait()
    some = back.at[pl.ds(0, NW - 1)]
    pltpu.make_async_copy(some, some, b_send).wait()
    pltpu.make_async_copy(home, home, b_recv).wait()


def settle(home, out, home_in, out_v, in_sem, out_sem):
    regions = NW // PARTS
    loads = [
        pltpu.make_async_copy(home.at[pl.ds(i * regions, regions)], home_in.at[pl.ds(i * regions, regions)], in_sem.at[i])
        for i in range(PARTS)
    ]
    stores = [
        pltpu.make_async_copy(
            out_v.at[:, pl.ds(i * regions * ROWS, regions * ROWS)],
            out.at[:, pl.ds(i * regions * ROWS, regions * ROWS)], out_sem.at[i])
        for i in range(PARTS)
    ]
    for load in loads:
        load.start()

    def pair(g, carry):
        v = home_in[pl.ds(2 * g, 2)].astype(F32)
        for h in range(2):
            u = v[:, :, h * MD:(h + 1) * MD, :]
            parts = [jnp.transpose(u[0], (1, 0, 2)), jnp.transpose(u[1], (1, 0, 2))]
            out_v[:, pl.ds(pl.multiple_of(g * 16, 16), 16), h * BLK:(h + 1) * BLK] = (
                jnp.concatenate(parts, axis=1).astype(BF16))
        return carry

    for i in range(PARTS):
        loads[i].wait()
        lax.fori_loop(i * regions // 2, (i + 1) * regions // 2, pair, 0, unroll=2)
        stores[i].start()
    for store in stores:
        store.wait()


def body(x, innov, obs_index, obs_weight, obs_list, tile_count, taper_class):
    anywhere = pl.BlockSpec(memory_space=pl.ANY)
    dma = pltpu.SemaphoreType.DMA
    home = pl.pallas_call(
        kernel,
        out_shape=jax.ShapeDtypeStruct((NW, ROWS, 16, BLK), BF16),
        in_specs=[pl.BlockSpec(memory_space=pltpu.HBM)] * 7,
        out_specs=anywhere,
        scratch_shapes=[
            pltpu.VMEM((MD, 256, Q), BF16),
            pltpu.VMEM((256 + 2, MD, Q), F32),
            pltpu.VMEM((2, 16, Q), BF16),
            pltpu.VMEM((2, 16, Q), BF16),
            pltpu.VMEM((2, 2, MD, BLK), F32),
            pltpu.VMEM((NW, ROWS, 16, BLK), BF16),
            pltpu.VMEM((NW, ROWS, 16, BLK), BF16),
            pltpu.VMEM((M, ROWS, Q), BF16),
            pltpu.VMEM((M, CAND), BF16),
            pltpu.VMEM((4, ROWS, Q), jnp.int32),
            pltpu.VMEM((4, ROWS, Q), F32),
            pltpu.VMEM((CELLS, BLK), F32),
            pltpu.VMEM((CELLS, CELLS), BF16),
            pltpu.VMEM((M, CELLS), BF16),
            pltpu.VMEM((CELLS, M), F32),
            pltpu.VMEM((CAND, M), BF16),
            pltpu.VMEM((5, BLK, BLK), F32),
            pltpu.VMEM((1, 16, 16), jnp.int32),
            pltpu.VMEM((1, 16, 16), jnp.int32),
            pltpu.SMEM((1, 16), jnp.int32),
            pltpu.VMEM((16, BLK), jnp.int32),
            pltpu.SMEM((16, BLK), jnp.int32),
            pltpu.VMEM((CELLS, Q), BF16),
            pltpu.VMEM((CELLS, Q), BF16),
            pltpu.VMEM((2 * HALO, Q), BF16),
            pltpu.VMEM((2 * HALO, Q), BF16),
            pltpu.VMEM((ROWS, M, Q), F32),
            pltpu.VMEM((NW, ROWS, 16, BLK), BF16),
            dma, dma((6,)), dma((2,)), dma((2,)), dma((CHUNKS,)), dma((CHUNKS,)),
            dma((2,)), dma((2,)), dma((2,)), dma((2,)), dma, dma, dma,
        ],
        compiler_params=pltpu.CompilerParams(
            collective_id=0, has_side_effects=True, vmem_limit_bytes=62 * 1024 * 1024),
    )(x, innov, obs_index, obs_weight, obs_list, tile_count, taper_class)
    return pl.pallas_call(
        settle,
        out_shape=jax.ShapeDtypeStruct((MD, 256, Q), BF16),
        in_specs=[anywhere],
        out_specs=anywhere,
        scratch_shapes=[
            pltpu.VMEM((NW, ROWS, 16, BLK), BF16),
            pltpu.VMEM((MD, 256, Q), BF16),
            dma((PARTS,)), dma((PARTS,)),
        ],
        compiler_params=pltpu.CompilerParams(vmem_limit_bytes=62 * 1024 * 1024),
    )(home)


def solution(mesh):
    in_specs = (
        P("wide", None, "lon"),
        P(None, "wide", "lon"),
        P(None, None, "lon"),
        P(None, None, "lon"),
        P("lon", "wide", None),
        P("lon", "wide"),
        P("lon", "wide", None),
    )
    return jax.shard_map(
        body, mesh=mesh, in_specs=in_specs, out_specs=P("wide", None, "lon"), check_vma=False)
```

```python
import functools

import jax
import jax.numpy as jnp
from jax import lax
from jax.experimental import pallas as pl
from jax.experimental.pallas import tpu as pltpu
from jax.sharding import PartitionSpec as P

MESH = pl.DeviceIdType.MESH
F32 = jnp.float32
BF16 = jnp.bfloat16

M = 256
ROWS = 8
Q = 256
NW = 32
NL = 8
MD = 8
BLK = 128
HALO = 512
CELLS = ROWS * Q
CAND = CELLS + 2 * HALO
CHUNKS = 2
PAIR = ROWS // CHUNKS
PARTS = 4
FIRST = 2
CHIPS = 16
STEP = 2
EARLY = 6
GROUP = 64


def iota(shape, dim):
    return lax.broadcasted_iota(jnp.int32, shape, dim)


def kernel(
    x_hbm, innov_hbm, idx_hbm, wgt_hbm, list_hbm, count_hbm, class_hbm, home,
    x_in, x_f, edge_out, edge_in, edge_f, sent, region, innov_in, innov_all, idx, wgt, cols, sel,
    dev, obs_acc, obs_all, table, listed, classes, count_s, dense_v, dense_s,
    own0, own1, out0, out1, part, back,
    x_sem, load_sem, edge_send, edge_recv, a_send, a_recv, ih_send, ih_recv, oh_send, oh_recv,
    b_send, b_recv, class_sem,
):
    me = lax.axis_index("wide")
    tile = lax.axis_index("lon")
    east = lax.rem(tile + 1, NL)
    west = lax.rem(tile + NL - 1, NL)
    core = lax.rem(me, 2)
    my_x = lax.rem(lax.div(me, 2), 4)
    my_y = lax.div(me, 8)

    def chip(k):
        def offset(i):
            return jnp.where(i == 0, 2, jnp.where(i == 3, 0, 2 * i - 1))

        to_y = lax.rem(my_y + offset(lax.div(k, 4)), 4)
        to_x = lax.rem(my_x + offset(lax.rem(k, 4)), 4)
        return to_y * 8 + to_x * 2

    first = pl.multiple_of(me * ROWS, ROWS)
    loads = [
        pltpu.make_async_copy(src, dst, load_sem.at[i]) for i, (src, dst) in enumerate((
            (idx_hbm.at[:, pl.ds(first, ROWS), :], idx),
            (wgt_hbm.at[:, pl.ds(first, ROWS), :], wgt),
            (innov_hbm, innov_in),
            (list_hbm, listed),
            (count_hbm, count_s),
            (class_hbm, classes),
        ))
    ]
    load_idx, load_wgt, load_innov, load_list, load_count, load_class = loads
    load_x = pltpu.make_async_copy(x_hbm, x_in, x_sem)
    load_x.start()

    barrier = pltpu.get_barrier_semaphore()

    def greet(k, carry):
        other = lax.rem(me + k, NW)
        pl.semaphore_signal(barrier, inc=1, device_id={"wide": other}, device_id_type=MESH)
        return carry

    for t in (east, west):
        pl.semaphore_signal(barrier, inc=1, device_id={"lon": t}, device_id_type=MESH)
    lax.fori_loop(1, NW, greet, 0)

    x_f[0] = jnp.zeros((MD, Q), F32)
    x_f[257] = jnp.zeros((MD, Q), F32)
    load_x.wait()
    for load in loads:
        load.start()

    def widen(g, carry):
        r0 = pl.multiple_of(g * 16, 16)
        v = x_in[:, pl.ds(r0, 16), :].astype(F32)
        lane = iota((MD, BLK), 1)
        firsts = jnp.zeros((MD, BLK), F32)
        lasts = jnp.zeros((MD, BLK), F32)
        for i in range(0, 16, 8):
            a = jnp.transpose(v[:, i:i + 8, :BLK], (1, 0, 2))
            b = jnp.transpose(v[:, i:i + 8, BLK:], (1, 0, 2))
            x_f[pl.ds(r0 + i + 1, 8)] = jnp.concatenate([a, b], axis=2)
            for j in range(8):
                k = i + j
                firsts = jnp.where(lane == k, pltpu.roll(a[j], k, 1) if k else a[j], firsts)
                lasts = jnp.where(lane == k, pltpu.roll(b[j], k + 1, 1), lasts)
        turns = lax.rem(g, 8) * 16
        wide_lane = iota((MD, Q), 1) - r0
        here = (wide_lane >= 0) & (wide_lane < 16)

        def place(new, old):
            new = pltpu.roll(new, turns, 1)
            return jnp.where(here, jnp.concatenate([new, new], axis=1), old)

        return place(firsts, carry[0]), place(lasts, carry[1])

    zeros = jnp.zeros((MD, Q), F32)
    left, right = lax.fori_loop(0, 16, widen, (zeros, zeros), unroll=4)
    edge_out[0] = jnp.concatenate([left, zeros], axis=0).astype(BF16)
    edge_out[1] = jnp.concatenate([right, zeros], axis=0).astype(BF16)

    pl.semaphore_wait(barrier, NW - 1 + 2)

    def lon_copy(src, dst, send_sem, recv_sem, t):
        copy = pltpu.make_async_remote_copy(
            src_ref=src, dst_ref=dst, send_sem=send_sem, recv_sem=recv_sem,
            device_id={"lon": t}, device_id_type=MESH)
        copy.start()
        return copy

    edges = [
        lon_copy(edge_out.at[side], edge_in.at[side], edge_send.at[side], edge_recv.at[side], t)
        for side, t in ((0, west), (1, east))
    ]

    load_idx.wait()
    load_wgt.wait()
    origin = me * CELLS

    entries = [(idx[k] - origin).astype(F32) for k in range(4)] + [wgt[k] for k in range(4)]
    entries = jnp.concatenate(entries + [jnp.zeros((BLK - 8 * ROWS, Q), F32)], axis=0)
    entries = jnp.transpose(entries, (1, 0))
    for i in range(ROWS):
        cols[i * Q:(i + 1) * Q, :] = pltpu.roll(entries, BLK - i, 1) if i else entries

    load_innov.wait()

    def turn(g, carry):
        m0 = pl.multiple_of(g * 16, 16)
        v = innov_in[pl.ds(m0, 16)].astype(F32)
        parts = [jnp.transpose(v[:8], (1, 0, 2)), jnp.transpose(v[8:], (1, 0, 2))]
        u = jnp.concatenate(parts, axis=1).astype(BF16)
        for r in range(ROWS):
            innov_all[pl.ds(m0, 16), HALO + r * Q:HALO + (r + 1) * Q] = u[r]
        return carry

    lax.fori_loop(0, M // 16, turn, 0)
    innov_halo = [
        lon_copy(innov_all.at[:, pl.ds(CELLS, HALO)], innov_all.at[:, pl.ds(0, HALO)],
                 ih_send.at[0], ih_recv.at[0], east),
        lon_copy(innov_all.at[:, pl.ds(HALO, HALO)], innov_all.at[:, pl.ds(HALO + CELLS, HALO)],
                 ih_send.at[1], ih_recv.at[1], west),
    ]

    d = (iota((BLK, BLK), 0) - iota((BLK, BLK), 1)).astype(F32)
    for c in range(4):
        s = d * (1.0 / (8.0 * 2.0 ** c))
        table[c] = (1.0 / (M - 1.0)) / (1.0 + s * s)
    table[4] = jnp.zeros((BLK, BLK), F32)

    for load in (load_list, load_count, load_class):
        load.wait()
    block = iota((16, BLK), 0)
    ids = iota((16, BLK), 1)
    counts = jnp.zeros((16, BLK), jnp.int32)
    for b in range(16):
        counts = jnp.where(block == b, count_s[0, b], counts)
    dense = jnp.full((16, BLK), 4, jnp.int32)
    for j in range(16):
        hit = (ids == listed[0, :, j:j + 1]) & (counts > j)
        dense = jnp.where(hit, classes[0, :, j:j + 1], dense)
    dense_v[...] = dense
    to_scalar = pltpu.make_async_copy(dense_v, dense_s, class_sem)
    to_scalar.start()

    def select(g, carry):
        o0 = pl.multiple_of(g * GROUP, GROUP)
        to = pl.multiple_of(lax.rem(o0 + HALO, CELLS), GROUP)
        here = cols[pl.ds(o0, GROUP), :]
        cell = [jnp.broadcast_to(here[:, 8 * k:8 * k + 1], (GROUP, BLK)) for k in range(4)]
        cell = [c.astype(jnp.int32).astype(jnp.int16) for c in cell]
        weight = [jnp.broadcast_to(here[:, 32 + 8 * k:33 + 8 * k], (GROUP, BLK)).astype(BF16) for k in range(4)]
        none = jnp.zeros((GROUP, BLK), BF16)
        sums = []
        for k in range(4):
            total = weight[k]
            for j in range(k):
                total = total + jnp.where(cell[j] == cell[k], weight[j], none)
            sums.append(total)
        lanes = iota((GROUP, BLK), 1).astype(jnp.int16)
        for t in range(CELLS // BLK):
            at = lanes + jnp.int16(t * BLK)
            value = jnp.where(at == cell[0], sums[0], none)
            for k in range(1, 4):
                value = jnp.where(at == cell[k], sums[k], value)
            sel[pl.ds(to, GROUP), t * BLK:(t + 1) * BLK] = value
        return carry

    steps = CELLS // GROUP
    lax.fori_loop(0, EARLY, select, 0, unroll=2)

    for copy in edges:
        copy.wait()
    for side in range(2):
        got = edge_in[side].astype(F32)
        for h in range(2):
            edge_f[side, h] = got[:MD, h * BLK:(h + 1) * BLK]

    def forecast(r):
        lane = iota((MD, BLK), 1)
        turns = lax.rem(BLK - lax.rem(r, 16) * 8, BLK)
        e_in = pltpu.roll(edge_f[0, lax.div(r, 16)], turns, 1)
        w_in = pltpu.roll(edge_f[1, lax.div(r, 16)], turns, 1)
        for i in range(ROWS):
            at = r * ROWS + i
            s, v, n = x_f[at], x_f[at + 1], x_f[at + 2]
            a, b = v[:, :BLK], v[:, BLK:]
            a_up, b_up = pltpu.roll(a, BLK - 1, 1), pltpu.roll(b, BLK - 1, 1)
            a_dn, b_dn = pltpu.roll(a, 1, 1), pltpu.roll(b, 1, 1)
            e_edge = pltpu.roll(e_in, BLK - 1 - i, 1)
            w_edge = pltpu.roll(w_in, BLK - i, 1) if i else w_in
            e_a = jnp.where(lane == BLK - 1, b_up, a_up)
            e_b = jnp.where(lane == BLK - 1, e_edge, b_up)
            w_a = jnp.where(lane == 0, w_edge, a_dn)
            w_b = jnp.where(lane == 0, a_dn, b_dn)
            halves = []
            for h, (c, e, w) in enumerate(((a, e_a, w_a), (b, e_b, w_b))):
                hs = slice(h * BLK, (h + 1) * BLK)
                halves.append(0.2 * (c + (n[:, hs] + s[:, hs])) + (0.5 * w - 0.1 * e))
            sent[r, i] = jnp.concatenate(halves, axis=0).astype(BF16)

    def send_forecast(other, j):
        rows = pl.ds(j * PAIR, PAIR)

        @pl.when(other == me)
        def _():
            pltpu.make_async_copy(sent.at[me, rows], region.at[me, rows], a_recv.at[j]).start()

        @pl.when(other != me)
        def _():
            pltpu.make_async_remote_copy(
                src_ref=sent.at[other, rows], dst_ref=region.at[me, rows],
                send_sem=a_send.at[j], recv_sem=a_recv.at[j],
                device_id={"wide": other}, device_id_type=MESH).start()

    def phase(c, carry):
        def compute_send(p, inner):
            others = [chip(STEP * p + i) + c for i in range(STEP)]
            for other in others:
                forecast(other)
            for other in others:
                send_forecast(other, 0)
            return inner

        lax.fori_loop(0, CHIPS // STEP, compute_send, 0)

        def send_rest(k, inner):
            for j in range(1, CHUNKS):
                send_forecast(chip(k) + c, j)
            return inner

        lax.fori_loop(0, CHIPS, send_rest, 0, unroll=4)
        return carry

    lax.fori_loop(0, 2, phase, 0)

    lax.fori_loop(EARLY, steps, select, 0, unroll=2)

    def anomaly(r, carry):
        v = region[:, r].astype(F32)
        for h in range(2):
            u = v[:, h * MD:(h + 1) * MD, :].reshape(M, BLK)
            u = u - jnp.sum(u, axis=0, keepdims=True) * (1.0 / M)
            dev[:, pl.ds(pl.multiple_of(r * Q + h * BLK, BLK), BLK)] = u.astype(BF16)
        return carry

    def lon_plan(src, dst, send_sem, recv_sem, t):
        return pltpu.make_async_remote_copy(
            src_ref=src, dst_ref=dst, send_sem=send_sem, recv_sem=recv_sem,
            device_id={"lon": t}, device_id_type=MESH)

    obs_halo = [
        lon_plan(obs_all.at[pl.ds(CELLS, HALO)], obs_all.at[pl.ds(0, HALO)],
                 oh_send.at[0], oh_recv.at[0], east),
        lon_plan(obs_all.at[pl.ds(HALO, HALO)], obs_all.at[pl.ds(HALO + CELLS, HALO)],
                 oh_send.at[1], oh_recv.at[1], west),
    ]
    obs_acc[...] = jnp.zeros((CELLS, M), F32)

    def product(block, j):
        at = pl.ds(pl.multiple_of(block * 2 * HALO, 2 * HALO), 2 * HALO)
        cells = pl.ds(pl.multiple_of(j * PAIR * Q, Q), PAIR * Q)
        total = obs_acc[at, :] + lax.dot_general(
            sel[at, cells], dev[:, cells], (((1,), (1,)), ((), ())), preferred_element_type=F32)
        obs_acc[at, :] = total
        some = total.astype(BF16)
        to = pl.multiple_of(jnp.where(block == 0, CELLS, 2 * HALO), HALO)
        obs_all[pl.ds(to, HALO), :] = some[:HALO]
        to = pl.multiple_of(jnp.where(block == 0, HALO, 3 * HALO), HALO)
        obs_all[pl.ds(to, HALO), :] = some[HALO:]

    def observe(step, carry):
        block = lax.div(step, CHUNKS)
        j = lax.rem(step, CHUNKS)

        @pl.when(block == 0)
        def _():
            arrived = region.at[:, pl.ds(j * PAIR, PAIR)]
            pltpu.make_async_copy(arrived, arrived, a_recv.at[j]).wait()
            lax.fori_loop(0, PAIR, lambda i, inner: anomaly(j * PAIR + i, inner), 0, unroll=2)

        product(block, j)

        @pl.when(step == CHUNKS - 1)
        def _():
            for copy in obs_halo:
                copy.start()

        return carry

    lax.fori_loop(0, 2 * CHUNKS, observe, 0)

    to_scalar.wait()

    def covariance(r, candidates, tapered):
        right = dev[:, pl.ds(r * Q if isinstance(r, int) else pl.multiple_of(r * Q, Q), Q)]
        for n, i in enumerate(candidates):
            cov = jnp.dot(obs_all[i * Q:(i + 1) * Q, :], right, preferred_element_type=F32)
            for oh in range(2):
                for ch in range(2):
                    factor = table[dense_s[2 * r + ch, 2 * i + oh]]
                    some = cov[oh * BLK:(oh + 1) * BLK, ch * BLK:(ch + 1) * BLK] * factor
                    tapered[n * Q + oh * BLK:n * Q + (oh + 1) * BLK, ch * BLK:(ch + 1) * BLK] = some.astype(BF16)

    def pipelined(pairs, cov, change, after):
        def step(p, carry):
            r = 2 * p
            change(r, 0)
            cov(r + 1, 1)
            change(r + 1, 1)
            cov(jnp.minimum(r + 2, ROWS - 1), 0)
            after(r)
            return carry

        lax.fori_loop(*pairs, step, 0)

    own = (own0, own1)

    def own_change(r, slot):
        part[r] = jnp.dot(innov_all[:, HALO:HALO + CELLS], own[slot][...], preferred_element_type=F32)

    outer = (out0, out1)

    def outer_change(r, slot):
        change = part[r] + jnp.dot(innov_all[:, 0:HALO], outer[slot][0:HALO, :], preferred_element_type=F32)
        change += jnp.dot(innov_all[:, HALO + CELLS:], outer[slot][HALO:, :], preferred_element_type=F32)
        state = region[:, r].astype(F32)
        parts = [
            state[:, h * MD:(h + 1) * MD, :] + change[:, h * BLK:(h + 1) * BLK].reshape(NW, MD, BLK)
            for h in range(2)
        ]
        back[:, r] = jnp.concatenate(parts, axis=1).astype(BF16)

    chip_columns = [lax.rem(my_x + offset, 4) * 2 for offset in (2, 1, 3, 0)]
    sibling = lax.div(me, 2) * 2 + 1 - core

    def send_pair(r):
        rows = pl.ds(r, 2)

        def send_back(other):
            pltpu.make_async_remote_copy(
                src_ref=back.at[other, rows], dst_ref=home.at[me, rows],
                send_sem=b_send, recv_sem=b_recv,
                device_id={"wide": other}, device_id_type=MESH).start()

        def send(k, carry):
            to_row = lax.rem(my_y + jnp.where(k == 0, 2, 2 * k - 1), 4) * 8
            for column in chip_columns:
                send_back(to_row + column)
                send_back(to_row + column + 1)
            return carry

        lax.fori_loop(0, 3, send, 0)
        for column in chip_columns[:3]:
            send_back(my_y * 8 + column)
            send_back(my_y * 8 + column + 1)
        send_back(sibling)
        pltpu.make_async_copy(back.at[me, rows], home.at[me, rows], b_recv).start()

    def own_covariance(r, slot):
        covariance(r, range(2, 10), own[slot])

    def outer_covariance(r, slot):
        covariance(r, (0, 1, 10, 11), outer[slot])

    own_covariance(0, 0)

    def update(late, carry):
        pairs = (late * FIRST, FIRST + late * (ROWS // 2 - FIRST))
        pipelined(pairs, own_covariance, own_change, lambda r: None)

        @pl.when(late == 0)
        def _():
            for copy in innov_halo + obs_halo:
                copy.wait()
            outer_covariance(0, 0)

        pipelined(pairs, outer_covariance, outer_change, send_pair)
        return carry

    lax.fori_loop(0, 2, update, 0)

    for j in range(CHUNKS):
        some = sent.at[pl.ds(0, NW - 1), pl.ds(j * PAIR, PAIR)]
        pltpu.make_async_copy(some, some, a_send.at[j]).wait()
    some = back.at[pl.ds(0, NW - 1)]
    pltpu.make_async_copy(some, some, b_send).wait()
    pltpu.make_async_copy(home, home, b_recv).wait()


def settle(home, out, home_in, out_v, in_sem, out_sem):
    regions = NW // PARTS
    loads = [
        pltpu.make_async_copy(home.at[pl.ds(i * regions, regions)], home_in.at[pl.ds(i * regions, regions)], in_sem.at[i])
        for i in range(PARTS)
    ]
    stores = [
        pltpu.make_async_copy(
            out_v.at[:, pl.ds(i * regions * ROWS, regions * ROWS)],
            out.at[:, pl.ds(i * regions * ROWS, regions * ROWS)], out_sem.at[i])
        for i in range(PARTS)
    ]
    for load in loads:
        load.start()

    def pair(g, carry):
        v = home_in[pl.ds(2 * g, 2)].astype(F32)
        for h in range(2):
            u = v[:, :, h * MD:(h + 1) * MD, :]
            parts = [jnp.transpose(u[0], (1, 0, 2)), jnp.transpose(u[1], (1, 0, 2))]
            out_v[:, pl.ds(pl.multiple_of(g * 16, 16), 16), h * BLK:(h + 1) * BLK] = (
                jnp.concatenate(parts, axis=1).astype(BF16))
        return carry

    for i in range(PARTS):
        loads[i].wait()
        lax.fori_loop(i * regions // 2, (i + 1) * regions // 2, pair, 0, unroll=2)
        stores[i].start()
    for store in stores:
        store.wait()


def body(x, innov, obs_index, obs_weight, obs_list, tile_count, taper_class):
    anywhere = pl.BlockSpec(memory_space=pl.ANY)
    dma = pltpu.SemaphoreType.DMA
    home = pl.pallas_call(
        kernel,
        out_shape=jax.ShapeDtypeStruct((NW, ROWS, 16, BLK), BF16),
        in_specs=[pl.BlockSpec(memory_space=pltpu.HBM)] * 7,
        out_specs=anywhere,
        scratch_shapes=[
            pltpu.VMEM((MD, 256, Q), BF16),
            pltpu.VMEM((256 + 2, MD, Q), F32),
            pltpu.VMEM((2, 16, Q), BF16),
            pltpu.VMEM((2, 16, Q), BF16),
            pltpu.VMEM((2, 2, MD, BLK), F32),
            pltpu.VMEM((NW, ROWS, 16, BLK), BF16),
            pltpu.VMEM((NW, ROWS, 16, BLK), BF16),
            pltpu.VMEM((M, ROWS, Q), BF16),
            pltpu.VMEM((M, CAND), BF16),
            pltpu.VMEM((4, ROWS, Q), jnp.int32),
            pltpu.VMEM((4, ROWS, Q), F32),
            pltpu.VMEM((CELLS, BLK), F32),
            pltpu.VMEM((CELLS, CELLS), BF16),
            pltpu.VMEM((M, CELLS), BF16),
            pltpu.VMEM((CELLS, M), F32),
            pltpu.VMEM((CAND, M), BF16),
            pltpu.VMEM((5, BLK, BLK), F32),
            pltpu.VMEM((1, 16, 16), jnp.int32),
            pltpu.VMEM((1, 16, 16), jnp.int32),
            pltpu.SMEM((1, 16), jnp.int32),
            pltpu.VMEM((16, BLK), jnp.int32),
            pltpu.SMEM((16, BLK), jnp.int32),
            pltpu.VMEM((CELLS, Q), BF16),
            pltpu.VMEM((CELLS, Q), BF16),
            pltpu.VMEM((2 * HALO, Q), BF16),
            pltpu.VMEM((2 * HALO, Q), BF16),
            pltpu.VMEM((ROWS, M, Q), F32),
            pltpu.VMEM((NW, ROWS, 16, BLK), BF16),
            dma, dma((6,)), dma((2,)), dma((2,)), dma((CHUNKS,)), dma((CHUNKS,)),
            dma((2,)), dma((2,)), dma((2,)), dma((2,)), dma, dma, dma,
        ],
        compiler_params=pltpu.CompilerParams(
            collective_id=0, has_side_effects=True, vmem_limit_bytes=62 * 1024 * 1024),
    )(x, innov, obs_index, obs_weight, obs_list, tile_count, taper_class)
    return pl.pallas_call(
        settle,
        out_shape=jax.ShapeDtypeStruct((MD, 256, Q), BF16),
        in_specs=[anywhere],
        out_specs=anywhere,
        scratch_shapes=[
            pltpu.VMEM((NW, ROWS, 16, BLK), BF16),
            pltpu.VMEM((MD, 256, Q), BF16),
            dma((PARTS,)), dma((PARTS,)),
        ],
        compiler_params=pltpu.CompilerParams(vmem_limit_bytes=62 * 1024 * 1024),
    )(home)


def solution(mesh):
    in_specs = (
        P("wide", None, "lon"),
        P(None, "wide", "lon"),
        P(None, None, "lon"),
        P(None, None, "lon"),
        P("lon", "wide", None),
        P("lon", "wide"),
        P("lon", "wide", None),
    )
    return jax.shard_map(
        body, mesh=mesh, in_specs=in_specs, out_specs=P("wide", None, "lon"), check_vma=False)
```
